512 devices in a mesh: head: 8 (over z), vocab: 64 (over x, y, core).
Axes of the slice: x: 4, y: 8, z: 8, core: 2. Of those that a mesh axis runs over, the one named last changes fastest.
Arguments:
- heads_out: bfloat16 [1024, 64, 128], P('vocab', 'head'), may hold values from -240 to 240, as said below
- unembed: bfloat16 [64, 128, 65536], P('head', None, 'vocab'), may hold values from -0.5 to 0.5
- targets: int32 [1024], replicated, may hold values from 0 to 65535
Outputs:
- log_probs: bfloat16 [1024, 65536], P('head', 'vocab')
- attribution: float32 [1024, 64], P(None, 'head')
The draws below stay inside these ranges and needn't reach their ends.
Inputs may be any that keep to these rules, and one draw needn't show every extreme that they name: heads_out is real-valued, each token scaled by its own positive factor.
All inputs are finite; a program needn't handle non-finite values.
Results may differ from the reference program's by a relative error of at most 0.001.
Values may be sent and summed in bfloat16 or wider, within the bound.
No kernel may reach another device: no remote copies, remote signals or barrier semaphores. Data moves between devices by JAX's collectives and lax.ppermute only.
A program may use at most 64 MiB of HBM per device.

```python
import jax
import jax.numpy as jnp

HEADS = 64
HD = 128
VOCAB = 65536
TOKENS = 1024


def draw_heads_out(key, part):
    key = jax.random.fold_in(key, 11)
    base_key, scale_key = jax.random.split(key)
    base = jnp.clip(jax.random.normal(base_key, (TOKENS, HEADS, HD), jnp.float32), -6.0, 6.0)
    logs = jax.random.uniform(scale_key, (TOKENS,), jnp.float32, jnp.log(0.5), jnp.log(2.0))
    return (base * jnp.exp(logs)[:, None, None]).astype(jnp.bfloat16)


def place_ends(drawn, own_key, smallest, high):
    longest = drawn.shape.index(max(drawn.shape))
    spots = []
    for shift in (0, 1):
        where = [jax.random.randint(jax.random.fold_in(own_key, axis), (), 0, length) for axis, length in enumerate(drawn.shape)]
        where[longest] = (where[longest] + shift) % drawn.shape[longest]
        spots.append(tuple(where))
    return drawn.at[spots[0]].set(smallest).at[spots[1]].set(high)


def steps_of(own_key, dims, shards, smallest, top_value):
    level = 1.0
    for dim, parts in shards:
        draws = jax.random.uniform(jax.random.fold_in(jax.random.fold_in(own_key, 6), dim), (parts,), jnp.float32, smallest / len(shards), top_value / len(shards))
        level = level * jnp.repeat(jnp.exp(draws), dims[dim] // parts).reshape((-1,) + (1,) * (len(dims) - 1 - dim))
    return level


def normal_values(own_key, extent, spread, bound, cuts=(), kind=jnp.bfloat16):
    factor_of = steps_of(own_key, extent, cuts, -0.22, 0.18) if cuts else 1.0
    drawn = jax.random.normal(own_key, extent, jnp.float32) * spread * factor_of
    return jnp.minimum(jnp.maximum(drawn, -bound), bound).astype(kind)


def setup_inputs(seed: int = 0) -> dict:
    arg_keys = jax.random.split(jax.random.key(seed), 4)
    return {
        "heads_out": draw_heads_out(jax.random.fold_in(arg_keys[3], 71), 0),
        "unembed": normal_values(arg_keys[1], (HEADS, HD, VOCAB), HD ** -0.5, 0.5, ((0, 8), (2, 64))),
        "targets": place_ends(jax.random.randint(arg_keys[2], (TOKENS,), 0, VOCAB), jax.random.fold_in(arg_keys[2], 1), 0, VOCAB - 1).astype(jnp.int32),
    }


def reference(heads_out, unembed, targets):
    flat = heads_out.reshape(TOKENS, HEADS * HD)
    logits = jnp.dot(flat, unembed.reshape(HEADS * HD, VOCAB), preferred_element_type=jnp.float32)
    picked = jnp.take(unembed, targets, axis=2)
    attribution = jnp.einsum("thd,hdt->th", heads_out.astype(jnp.float32), picked.astype(jnp.float32))
    top = jnp.max(logits, axis=1, keepdims=True)
    total = jnp.sum(jnp.exp(logits - top), axis=1, keepdims=True)
    log_probs = (logits - top - jnp.log(total)).astype(jnp.bfloat16)
    return log_probs, attribution
```

```python
import jax
import jax.numpy as jnp
from jax import lax
from jax.sharding import PartitionSpec as P

NX, NY, NC, NZ = 4, 8, 2, 8
SCALE = 0.125


def vocab_index(x, y, c):
    return (x * NY + y) * NC + c


Y_GROUPS = [[vocab_index(x, y, c) for y in range(NY)] for x in range(NX) for c in range(NC)]
X_GROUPS = [[vocab_index(x, y, c) for x in range(NX)] for y in range(NY) for c in range(NC)]
CORE_SWAP = [(v, v ^ 1) for v in range(NX * NY * NC)]
UP = [(z, (z + 1) % NZ) for z in range(NZ)]
DOWN = [(z, (z - 1) % NZ) for z in range(NZ)]


def share(block, groups, count):
    copies = jnp.broadcast_to(block[None], (count,) + block.shape)
    return lax.all_to_all(copies, "vocab", 0, 0, axis_index_groups=groups, tiled=True)


def coded(values):
    return (values * SCALE).astype(jnp.float16)


def decoded(values):
    return values.astype(jnp.float32) * (1.0 / SCALE)


def cores_in_order(values, core):
    pair = values.reshape((NC, -1) + values.shape[1:])
    return jnp.where(core == 0, pair, pair[::-1]).reshape(values.shape)


def on_device(heads_out, unembed, targets):
    per_device, heads, hd = heads_out.shape
    depth = heads * hd
    slab = unembed.shape[2]
    half = slab // 2
    weights = unembed.reshape(depth, slab)
    vocab_id = lax.axis_index("vocab")
    z = lax.axis_index("head")
    core = vocab_id % NC

    column = share(heads_out.reshape(per_device, depth), Y_GROUPS, NY)
    own = share(column, X_GROUPS, NX)
    other = lax.ppermute(own, "vocab", CORE_SWAP)
    rows = jnp.stack([own, other])
    rows = rows.reshape(2, NZ, NY // 2 * per_device, depth)

    def partial_logits(target):
        part = lax.dynamic_slice_in_dim(rows, target % NZ, 1, axis=1)[:, 0]
        return lax.dot_general(
            part.reshape(-1, depth), weights, (((1,), (0,)), ((), ())), preferred_element_type=jnp.float32
        )

    far = coded(partial_logits(z + 4))
    up = lax.ppermute(far[:, :half], "head", UP)
    down = lax.ppermute(far[:, half:], "head", DOWN)
    nothing = jnp.zeros((far.shape[0], half), jnp.float32)
    up = jnp.concatenate([decoded(up), nothing], axis=1)
    down = jnp.concatenate([nothing, decoded(down)], axis=1)
    for distance in (3, 2, 1):
        up = lax.ppermute(coded(partial_logits(z + distance) + up), "head", UP)
        down = lax.ppermute(coded(partial_logits(z - distance + NZ) + down), "head", DOWN)
        up, down = decoded(up), decoded(down)
    logits = partial_logits(z) + up + down

    ids = targets.reshape(NX, NY, NC, per_device)
    ids = jnp.where(core == 0, ids, ids[:, :, ::-1])
    ids = ids.transpose(2, 0, 1, 3).reshape(-1) - vocab_id * slab
    chosen = (ids[:, None] == jnp.arange(slab)[None, :]).astype(jnp.bfloat16)
    picked = lax.dot_general(chosen, weights, (((1,), (1,)), ((), ())), preferred_element_type=jnp.float32)
    terms = rows.reshape(-1, heads, hd).astype(jnp.float32) * picked.reshape(-1, heads, hd)
    terms = jnp.sum(terms, axis=-1).reshape(NC, NX, NY, per_device * heads)
    terms = jnp.where(core == 0, terms, terms[::-1])
    terms = terms.transpose(1, 2, 0, 3).reshape(NX * NY * NC, per_device * heads)
    own_terms = jnp.sum(lax.all_to_all(terms, "vocab", 0, 0, tiled=True), axis=0)

    top = jnp.max(logits, axis=1, keepdims=True)
    lse = top[:, 0] + jnp.log(jnp.sum(jnp.exp(logits - top), axis=1))
    message = jnp.stack([cores_in_order(lse, core), own_terms])
    messages = share(message, None, NX * NY * NC)
    every_lse, attribution = messages[:, 0], messages[:, 1]
    top = jnp.max(every_lse, axis=0)
    lse = top + jnp.log(jnp.sum(jnp.exp(every_lse - top[None]), axis=0))
    lse = cores_in_order(lse, core)
    log_probs = cores_in_order((logits - lse[:, None]).astype(jnp.bfloat16), core)
    log_probs = log_probs.reshape(NC, NY // 2, per_device, slab)
    log_probs = log_probs.transpose(1, 0, 2, 3).reshape(-1, slab)
    return (log_probs, attribution.reshape(-1, heads))


def solution(mesh):
    in_specs = (P("vocab", "head", None), P("head", None, "vocab"), P())
    out_specs = (P("head", "vocab"), P(None, "head"))
    return jax.shard_map(
        on_device, mesh=mesh, in_specs=in_specs, out_specs=out_specs, check_vma=False
    )
```

```python
import functools

import jax
import jax.numpy as jnp
from jax import lax
from jax.experimental import pallas as pl
from jax.experimental.pallas import tpu as pltpu
from jax.sharding import PartitionSpec as P

NX, NY, NC, NZ = 4, 8, 2, 8
NV = NX * NY * NC
SCALE = 0.125
MIB = 2**20
SLOT_OF = {5: 0, 4: 1, 2: 2, 3: 3, 7: 4, 6: 5, 1: 6, 0: 7}


def vocab_index(x, y, c):
    return (x * NY + y) * NC + c


Y_GROUPS = [[vocab_index(x, y, c) for y in range(NY)] for x in range(NX) for c in range(NC)]
X_GROUPS = [[vocab_index(x, y, c) for x in range(NX)] for y in range(NY) for c in range(NC)]
CORE_MAJOR = [[vocab_index(x, y, c) for c in range(NC) for x in range(NX) for y in range(NY)]]
CORE_SWAP = [(v, v ^ 1) for v in range(NV)]


def matching(sign):
    pairs = []
    for z in range(NZ):
        for v in range(NV):
            step = sign if (z + v) % 2 == 0 else -sign
            pairs.append((z * NV + v, (z + step) % NZ * NV + v))
    return pairs


FIRST, SECOND = matching(1), matching(-1)


def share(block, groups, count):
    copies = jnp.broadcast_to(block[None], (count,) + block.shape)
    return lax.all_to_all(copies, "vocab", 0, 0, axis_index_groups=groups, tiled=True)


def coded(values):
    return (values * SCALE).astype(jnp.float16)


def decoded(values):
    return values.astype(jnp.float32) * (1.0 / SCALE)


def ring(values, pairs):
    return lax.ppermute(values, ("head", "vocab"), pairs)


def tied(value, earlier):
    return lax.optimization_barrier((value, earlier))[0]


def cost(flops, mib):
    return pl.CostEstimate(flops=flops, bytes_accessed=mib * MIB, transcendentals=0)


def params():
    return pltpu.CompilerParams(vmem_limit_bytes=32 * MIB)


SMEM = pl.BlockSpec(memory_space=pltpu.SMEM)
VMEM = pl.BlockSpec(memory_space=pltpu.VMEM)


def pick_kernel(per_device, place_ref, ids_ref, weights_ref, own_ref, other_ref):
    tokens, slab = ids_ref.shape[0], weights_ref.shape[1]
    core = place_ref[1]
    lanes = lax.broadcasted_iota(jnp.int32, (tokens, slab), 1)
    chosen = (ids_ref[...] == lanes).astype(jnp.float32).astype(jnp.bfloat16)
    picked = lax.dot_general(
        chosen, weights_ref[...], (((1,), (1,)), ((), ())), preferred_element_type=jnp.float32
    ).astype(jnp.bfloat16)
    for place in range(tokens // per_device // NC):
        first = picked[2 * place * per_device : (2 * place + 1) * per_device]
        second = picked[(2 * place + 1) * per_device : (2 * place + 2) * per_device]
        rows = slice(place * per_device, (place + 1) * per_device)
        own_ref[rows] = jnp.where(core == 0, first, second)
        other_ref[rows] = jnp.where(core == 0, second, first)


def pick_columns(place, ids, weights, per_device):
    depth, slab = weights.shape
    tokens = ids.shape[0]
    block = 256
    half = jax.ShapeDtypeStruct((tokens // NC, depth), jnp.bfloat16)
    return pl.pallas_call(
        functools.partial(pick_kernel, per_device),
        grid=(tokens // block,),
        in_specs=[
            SMEM,
            pl.BlockSpec((block, 1), lambda i: (i, 0)),
            pl.BlockSpec((depth, slab), lambda i: (0, 0)),
        ],
        out_specs=[pl.BlockSpec((block // NC, depth), lambda i: (i, 0))] * 2,
        out_shape=[half, half],
        cost_estimate=cost(2 * tokens * depth * slab, 8),
        compiler_params=params(),
    )(place, ids, weights)


def products_kernel(heads, per_device, kind, place_ref, rows_ref, picked_ref, weights_ref, *rest):
    earlier_ref = rest[0] if kind else None
    sums_ref, terms_ref = rest[kind:]
    z, core, way = place_ref[0], place_ref[1], place_ref[2]
    depth = rows_ref.shape[1]
    lanes = heads * per_device
    head_of = lax.broadcasted_iota(jnp.int32, (depth, lanes), 0) // (depth // heads)
    lane_head = lax.broadcasted_iota(jnp.int32, (depth, lanes), 1) % heads
    spread = (head_of == lane_head).astype(jnp.float32).astype(jnp.bfloat16)
    block = rows_ref.shape[0] // NZ
    step = 2 * block
    places = step // per_device
    token = lax.broadcasted_iota(jnp.int32, (places, per_device, lanes), 1)
    lane_token = lax.broadcasted_iota(jnp.int32, (places, per_device, lanes), 2) // heads

    def slot(target):
        distance = jnp.bitwise_and((target - z) * way, NZ - 1)
        found = jnp.int32(0)
        for key, value in SLOT_OF.items():
            found = jnp.where(distance == key, value, found)
        return found

    def body(i, carry):
        rows = rows_ref[pl.ds(i * step, step)]
        sums = jnp.dot(rows, weights_ref[...], preferred_element_type=jnp.float32)
        for part in range(2):
            sums_ref[slot(2 * i + part)] = sums[part * block : (part + 1) * block]
        products = rows.astype(jnp.float32) * picked_ref[pl.ds(i * step, step)].astype(jnp.float32)
        high = products.astype(jnp.bfloat16)
        low = (products - high.astype(jnp.float32)).astype(jnp.bfloat16)
        terms = jnp.dot(high, spread, preferred_element_type=jnp.float32)
        terms += jnp.dot(low, spread, preferred_element_type=jnp.float32)
        terms = jnp.where(token == lane_token, terms.reshape(places, per_device, lanes), 0.0)
        terms = jnp.sum(terms, axis=1)
        if kind == 0:
            terms_ref[pl.ds(i * places, places)] = terms
        else:
            terms_ref[1 - core, pl.ds(i * places, places), 0] = terms
        return carry

    lax.fori_loop(0, rows_ref.shape[0] // step, body, 0)
    if kind == 1:
        terms_ref[core, :, 0] = earlier_ref[...]


def products(place, rows, picked, weights, heads, per_device, earlier=None):
    tokens, depth = rows.shape
    slab = weights.shape[1]
    lanes = heads * per_device
    places = tokens // per_device
    kind = 0 if earlier is None else 1
    shape = (places, lanes) if kind == 0 else (NC, places, 1, lanes)
    return pl.pallas_call(
        functools.partial(products_kernel, heads, per_device, kind),
        in_specs=[SMEM, VMEM, VMEM, VMEM] + [VMEM] * kind,
        out_specs=[VMEM, VMEM],
        out_shape=[
            jax.ShapeDtypeStruct((NZ, tokens // NZ, slab), jnp.float32),
            jax.ShapeDtypeStruct(shape, jnp.float32),
        ],
        cost_estimate=cost(2 * tokens * depth * (slab + 4 * lanes), 6),
        compiler_params=params(),
    )(place, rows, picked, weights, *([] if earlier is None else [earlier]))


def eye(size):
    rows = lax.broadcasted_iota(jnp.int32, (size, size), 0)
    return rows == lax.broadcasted_iota(jnp.int32, (size, size), 1)


def stats_kernel(place_ref, own_ref, other_ref, terms_ref, message_ref):
    core = place_ref[1]
    found = []
    for ref in (own_ref, other_ref):
        logits = ref[...]
        top = jnp.max(logits, axis=1, keepdims=True)
        found.append(top + jnp.log(jnp.sum(jnp.exp(logits - top), axis=1, keepdims=True)))
    own, other = found
    lse = jnp.concatenate([jnp.where(core == 0, own, other), jnp.where(core == 0, other, own)], axis=0)
    size = lse.shape[0]
    lse = jnp.sum(jnp.where(eye(size), lse, 0.0), axis=0, keepdims=True)
    terms = jnp.sum(terms_ref[...], axis=0)
    message = jnp.concatenate([lse, terms], axis=0)
    message_ref[...] = jnp.broadcast_to(message[None], message_ref.shape)


def stats(place, own, other, terms):
    size = own.shape[0] + other.shape[0]
    return pl.pallas_call(
        stats_kernel,
        in_specs=[SMEM, VMEM, VMEM, VMEM],
        out_specs=VMEM,
        out_shape=jax.ShapeDtypeStruct((NV, 2, size), jnp.float32),
        cost_estimate=cost(0, 1),
        compiler_params=params(),
    )(place, own, other, terms)


def finish_kernel(heads, per_device, place_ref, own_ref, other_ref, messages_ref, out_ref, attribution_ref):
    core = place_ref[1]
    every = messages_ref[:, 0, :]
    size = every.shape[1]
    top = jnp.max(every, axis=0, keepdims=True)
    lse = top + jnp.log(jnp.sum(jnp.exp(every - top), axis=0, keepdims=True))
    lse = jnp.sum(jnp.where(eye(size), lse, 0.0), axis=1, keepdims=True)
    half = size // NC
    for c in range(NC):
        logits = jnp.where(core == c, own_ref[...], other_ref[...])
        values = (logits - lse[c * half : (c + 1) * half]).astype(out_ref.dtype)
        for place in range(half // per_device):
            start = (place * NC + c) * per_device
            out_ref[start : start + per_device] = values[place * per_device : (place + 1) * per_device]
    terms = messages_ref[:, 1, :]
    shape = (NV, per_device, size)
    token = lax.broadcasted_iota(jnp.int32, shape, 1)
    lane_token = lax.broadcasted_iota(jnp.int32, shape, 2) // heads
    terms = jnp.where(token == lane_token, jnp.broadcast_to(terms[:, None, :], shape), 0.0)
    head = lax.broadcasted_iota(jnp.int32, (heads, size), 0)
    lane_head = lax.broadcasted_iota(jnp.int32, (heads, size), 1) % heads
    attribution_ref[...] = lax.dot_general(
        (head == lane_head).astype(jnp.float32),
        terms.reshape(NV * per_device, size),
        (((1,), (1,)), ((), ())),
        preferred_element_type=jnp.float32,
        precision=lax.Precision.HIGHEST,
    )


def finish(place, own, other, messages, heads, per_device):
    tokens, slab = own.shape[0] + other.shape[0], own.shape[1]
    return pl.pallas_call(
        functools.partial(finish_kernel, heads, per_device),
        in_specs=[SMEM, VMEM, VMEM, VMEM],
        out_specs=[VMEM, VMEM],
        out_shape=[
            jax.ShapeDtypeStruct((tokens, slab), jnp.bfloat16),
            jax.ShapeDtypeStruct((heads, NV * per_device), jnp.float32),
        ],
        cost_estimate=cost(0, 1),
        compiler_params=params(),
    )(place, own, other, messages)


def on_device(heads_out, unembed, targets):
    per_device, heads, hd = heads_out.shape
    depth = heads * hd
    slab = unembed.shape[2]
    weights = unembed.reshape(depth, slab)
    vocab_id = lax.axis_index("vocab")
    z = lax.axis_index("head")
    core = vocab_id & 1
    way = 1 - 2 * ((z + core) & 1)
    place = jnp.stack([z, core, way])
    ids = (targets - vocab_id * slab).reshape(-1, 1)
    picked_own, picked_other = pick_columns(place, ids, weights, per_device)

    column = share(heads_out.reshape(per_device, depth), Y_GROUPS, NY)
    own = share(column, X_GROUPS, NX)
    other = lax.ppermute(own, "vocab", CORE_SWAP).reshape(-1, depth)
    sums_a, terms = products(place, own.reshape(-1, depth), picked_own, weights, heads, per_device)
    a = coded(sums_a[0:2])
    got_a = ring(a, SECOND)
    sums_b, terms = products(place, tied(other, a), picked_other, weights, heads, per_device, terms)
    b = coded(sums_b[0:2])
    got_b = ring(b, SECOND)

    a = coded(sums_a[2:4] + decoded(tied(got_a, b)))
    got_a = ring(a, FIRST)
    b = coded(sums_b[2:4] + decoded(tied(got_b, a)))
    got_b = ring(b, FIRST)
    terms = tied(terms, b).reshape(NV, 1, per_device * heads)
    terms = lax.all_to_all(terms, "vocab", 0, 0, axis_index_groups=CORE_MAJOR, tiled=True)
    a = coded(sums_a[4:6] + decoded(tied(got_a, b)))
    got_a = ring(a, SECOND)
    b = coded(sums_b[4:6] + decoded(tied(got_b, a)))
    got_b = ring(b, SECOND)
    got_a = decoded(tied(got_a, b))
    a = coded(sums_a[6] + got_a[1])
    last_a = ring(a, FIRST)
    got_b = decoded(tied(got_b, a))
    b = coded(sums_b[6] + got_b[1])
    last_b = ring(b, FIRST)
    own_logits = sums_a[7] + got_a[0] + decoded(tied(last_a, b))
    other_logits = sums_b[7] + got_b[0] + decoded(last_b)

    message = stats(place, own_logits, other_logits, terms)
    messages = lax.all_to_all(message, "vocab", 0, 0, tiled=True)
    log_probs, attribution = finish(place, own_logits, other_logits, messages, heads, per_device)
    return (log_probs, attribution.T)


def solution(mesh):
    in_specs = (P("vocab", "head", None), P("head", None, "vocab"), P())
    out_specs = (P("head", "vocab"), P(None, "head"))
    return jax.shard_map(
        on_device, mesh=mesh, in_specs=in_specs, out_specs=out_specs, check_vma=False
    )
```

```python
import functools

import jax
import jax.numpy as jnp
from jax import lax
from jax.experimental import pallas as pl
from jax.experimental.pallas import tpu as pltpu
from jax.sharding import PartitionSpec as P

NX, NY, NC, NZ = 4, 8, 2, 8
NV = NX * NY * NC
SCALE = 0.125
MIB = 2**20
SLOT_OF = {4: 0, 5: 1, 3: 2, 6: 3, 2: 4, 7: 5, 1: 6, 0: 7}


def vocab_index(x, y, c):
    return (x * NY + y) * NC + c


Y_GROUPS = [[vocab_index(x, y, c) for y in range(NY)] for x in range(NX) for c in range(NC)]
X_GROUPS = [[vocab_index(x, y, c) for x in range(NX)] for y in range(NY) for c in range(NC)]
CORE_MAJOR = [[vocab_index(x, y, c) for c in range(NC) for x in range(NX) for y in range(NY)]]
CORE_SWAP = [(v, v ^ 1) for v in range(NV)]


def hop(sign):
    pairs = []
    for z in range(NZ):
        for v in range(NV):
            step = sign if v % NC == 0 else -sign
            pairs.append((z * NV + v, (z + step) % NZ * NV + v))
    return pairs


AHEAD, BACK, AHEAD_TWO, BACK_TWO = hop(1), hop(-1), hop(2), hop(-2)


def share(block, groups, count):
    copies = jnp.broadcast_to(block[None], (count,) + block.shape)
    return lax.all_to_all(copies, "vocab", 0, 0, axis_index_groups=groups, tiled=True)


def coded(values):
    return (values * SCALE).astype(jnp.float16)


def decoded(values):
    return values.astype(jnp.float32) * (1.0 / SCALE)


def ring(values, pairs):
    return lax.ppermute(values, ("head", "vocab"), pairs)


def tied(value, earlier):
    return lax.optimization_barrier((value, earlier))[0]


def cost(flops, mib):
    return pl.CostEstimate(flops=flops, bytes_accessed=mib * MIB, transcendentals=0)


def params():
    return pltpu.CompilerParams(vmem_limit_bytes=20 * MIB)


SMEM = pl.BlockSpec(memory_space=pltpu.SMEM)
VMEM = pl.BlockSpec(memory_space=pltpu.VMEM)


def pick_kernel(per_device, place_ref, ids_ref, weights_ref, own_ref, other_ref):
    tokens, slab = ids_ref.shape[0], weights_ref.shape[1]
    core = place_ref[1]
    lanes = lax.broadcasted_iota(jnp.int32, (tokens, slab), 1)
    chosen = (ids_ref[...] == lanes).astype(jnp.float32).astype(jnp.bfloat16)
    picked = lax.dot_general(
        chosen, weights_ref[...], (((1,), (1,)), ((), ())), preferred_element_type=jnp.float32
    ).astype(jnp.bfloat16)
    for place in range(tokens // per_device // NC):
        first = picked[2 * place * per_device : (2 * place + 1) * per_device]
        second = picked[(2 * place + 1) * per_device : (2 * place + 2) * per_device]
        rows = slice(place * per_device, (place + 1) * per_device)
        own_ref[rows] = jnp.where(core == 0, first, second)
        other_ref[rows] = jnp.where(core == 0, second, first)


def pick_columns(place, ids, weights, per_device):
    depth, slab = weights.shape
    tokens = ids.shape[0]
    block = 256
    half = jax.ShapeDtypeStruct((tokens // NC, depth), jnp.bfloat16)
    return pl.pallas_call(
        functools.partial(pick_kernel, per_device),
        grid=(tokens // block,),
        in_specs=[
            SMEM,
            pl.BlockSpec((block, 1), lambda i: (i, 0)),
            pl.BlockSpec((depth, slab), lambda i: (0, 0)),
        ],
        out_specs=[pl.BlockSpec((block // NC, depth), lambda i: (i, 0))] * 2,
        out_shape=[half, half],
        cost_estimate=cost(2 * tokens * depth * slab, 8),
        compiler_params=params(),
    )(place, ids, weights)


def sums_kernel(kind, place_ref, rows_ref, weights_ref, *rest):
    sums_ref = rest[-1]
    z, way = place_ref[0], place_ref[2]
    block = sums_ref.shape[2]
    parts = rows_ref.shape[0] // block
    sums = jnp.dot(rows_ref[...], weights_ref[...], preferred_element_type=jnp.float32)
    for part in range(parts):
        target = pl.program_id(0) * parts + part
        distance = jnp.bitwise_and((target - z) * way, NZ - 1)
        slot = jnp.int32(0)
        for key, value in SLOT_OF.items():
            slot = jnp.where(distance == key, value, slot)
        sums_ref[slot, kind] = sums[part * block : (part + 1) * block]


def partial_sums(place, rows, weights, earlier=None):
    tokens, depth = rows.shape
    slab = weights.shape[1]
    steps = 2
    kind = 0 if earlier is None else 1
    return pl.pallas_call(
        functools.partial(sums_kernel, kind),
        grid=(steps,),
        in_specs=[SMEM, pl.BlockSpec((tokens // steps, depth), lambda i: (i, 0)), VMEM] + [VMEM] * kind,
        out_specs=VMEM,
        out_shape=jax.ShapeDtypeStruct((NZ, NC, tokens // NZ, slab), jnp.float32),
        input_output_aliases={3: 0} if kind else {},
        cost_estimate=cost(2 * tokens * depth * slab, 6),
        compiler_params=params(),
    )(place, rows, weights, *([earlier] if kind else []))


def terms_kernel(heads, per_device, place_ref, own_ref, other_ref, picked_own_ref, picked_other_ref, terms_ref):
    core = place_ref[1]
    tokens, depth = own_ref.shape
    lanes = heads * per_device
    places = tokens // per_device
    head_of = lax.broadcasted_iota(jnp.int32, (depth, lanes), 0) // (depth // heads)
    lane_head = lax.broadcasted_iota(jnp.int32, (depth, lanes), 1) % heads
    spread = (head_of == lane_head).astype(jnp.float32).astype(jnp.bfloat16)
    token = lax.broadcasted_iota(jnp.int32, (places, per_device, lanes), 1)
    lane_token = lax.broadcasted_iota(jnp.int32, (places, per_device, lanes), 2) // heads
    parts = []
    for rows_ref, picked_ref in ((own_ref, picked_own_ref), (other_ref, picked_other_ref)):
        products = rows_ref[...].astype(jnp.float32) * picked_ref[...].astype(jnp.float32)
        high = products.astype(jnp.bfloat16)
        parts += [high, (products - high.astype(jnp.float32)).astype(jnp.bfloat16)]
    sums = jnp.dot(jnp.concatenate(parts, axis=0), spread, preferred_element_type=jnp.float32)
    for kind in range(NC):
        start = 2 * kind * tokens
        terms = sums[start : start + tokens] + sums[start + tokens : start + 2 * tokens]
        terms = jnp.where(token == lane_token, terms.reshape(places, per_device, lanes), 0.0)
        terms_ref[jnp.bitwise_xor(core, kind), :, 0] = jnp.sum(terms, axis=1)


def head_terms(place, own, other, picked_own, picked_other, heads, per_device):
    tokens, depth = own.shape
    lanes = heads * per_device
    steps = 2
    rows = pl.BlockSpec((tokens // steps, depth), lambda i: (i, 0))
    places = tokens // per_device
    return pl.pallas_call(
        functools.partial(terms_kernel, heads, per_device),
        grid=(steps,),
        in_specs=[SMEM, rows, rows, rows, rows],
        out_specs=pl.BlockSpec((NC, places // steps, 1, lanes), lambda i: (0, i, 0, 0)),
        out_shape=jax.ShapeDtypeStruct((NC, places, 1, lanes), jnp.float32),
        cost_estimate=cost(16 * tokens * depth * lanes, 4),
        compiler_params=params(),
    )(place, own, other, picked_own, picked_other)


def eye(size):
    rows = lax.broadcasted_iota(jnp.int32, (size, size), 0)
    return rows == lax.broadcasted_iota(jnp.int32, (size, size), 1)


def stats_kernel(place_ref, logits_ref, terms_ref, message_ref):
    core = place_ref[1]
    found = []
    for kind in range(NC):
        logits = logits_ref[kind]
        top = jnp.max(logits, axis=1, keepdims=True)
        found.append(top + jnp.log(jnp.sum(jnp.exp(logits - top), axis=1, keepdims=True)))
    own, other = found
    lse = jnp.concatenate([jnp.where(core == 0, own, other), jnp.where(core == 0, other, own)], axis=0)
    size = lse.shape[0]
    lse = jnp.sum(jnp.where(eye(size), lse, 0.0), axis=0, keepdims=True)
    terms = jnp.sum(terms_ref[...], axis=0)
    message = jnp.concatenate([lse, terms], axis=0)
    message_ref[...] = jnp.broadcast_to(message[None], message_ref.shape)


def stats(place, logits, terms):
    size = NC * logits.shape[1]
    return pl.pallas_call(
        stats_kernel,
        in_specs=[SMEM, VMEM, VMEM],
        out_specs=VMEM,
        out_shape=jax.ShapeDtypeStruct((NV, 2, size), jnp.float32),
        cost_estimate=cost(0, 1),
        compiler_params=params(),
    )(place, logits, terms)


def finish_kernel(heads, per_device, place_ref, logits_ref, messages_ref, out_ref, attribution_ref):
    core = place_ref[1]
    every = messages_ref[:, 0, :]
    size = every.shape[1]
    top = jnp.max(every, axis=0, keepdims=True)
    lse = top + jnp.log(jnp.sum(jnp.exp(every - top), axis=0, keepdims=True))
    lse = jnp.sum(jnp.where(eye(size), lse, 0.0), axis=1, keepdims=True)
    half = size // NC
    for c in range(NC):
        logits = logits_ref[jnp.bitwise_xor(core, c)]
        values = (logits - lse[c * half : (c + 1) * half]).astype(out_ref.dtype)
        for place in range(half // per_device):
            start = (place * NC + c) * per_device
            out_ref[start : start + per_device] = values[place * per_device : (place + 1) * per_device]
    terms = messages_ref[:, 1, :]
    shape = (NV, per_device, size)
    token = lax.broadcasted_iota(jnp.int32, shape, 1)
    lane_token = lax.broadcasted_iota(jnp.int32, shape, 2) // heads
    terms = jnp.where(token == lane_token, jnp.broadcast_to(terms[:, None, :], shape), 0.0)
    head = lax.broadcasted_iota(jnp.int32, (heads, size), 0)
    lane_head = lax.broadcasted_iota(jnp.int32, (heads, size), 1) % heads
    attribution_ref[...] = lax.dot_general(
        (head == lane_head).astype(jnp.float32),
        terms.reshape(NV * per_device, size),
        (((1,), (1,)), ((), ())),
        preferred_element_type=jnp.float32,
        precision=lax.Precision.HIGHEST,
    )


def finish(place, logits, messages, heads, per_device):
    tokens, slab = NC * logits.shape[1], logits.shape[2]
    return pl.pallas_call(
        functools.partial(finish_kernel, heads, per_device),
        in_specs=[SMEM, VMEM, VMEM],
        out_specs=[VMEM, VMEM],
        out_shape=[
            jax.ShapeDtypeStruct((tokens, slab), jnp.bfloat16),
            jax.ShapeDtypeStruct((heads, NV * per_device), jnp.float32),
        ],
        cost_estimate=cost(0, 1),
        compiler_params=params(),
    )(place, logits, messages)


def on_device(heads_out, unembed, targets):
    per_device, heads, hd = heads_out.shape
    depth = heads * hd
    slab = unembed.shape[2]
    weights = unembed.reshape(depth, slab)
    vocab_id = lax.axis_index("vocab")
    z = lax.axis_index("head")
    core = vocab_id & 1
    way = 1 - 2 * core
    place = jnp.stack([z, core, way])
    ids = (targets - vocab_id * slab).reshape(-1, 1)
    picked_own, picked_other = pick_columns(place, ids, weights, per_device)
    column = share(heads_out.reshape(per_device, depth), Y_GROUPS, NY)
    own = share(column, X_GROUPS, NX).reshape(-1, depth)
    own = tied(own, picked_own)
    other = lax.ppermute(own, "vocab", CORE_SWAP)
    sums = partial_sums(place, own, weights)
    sums = partial_sums(place, tied(other, sums), weights, sums)

    sent = coded(sums[0])
    four = ring(sent, AHEAD_TWO)
    sent = coded(tied(sums, sent)[1])
    five = ring(sent, BACK)
    sent = coded(tied(sums, sent)[2])
    three = ring(sent, AHEAD)
    terms = head_terms(place, own, tied(other, sent), picked_own, picked_other, heads, per_device)
    sent = coded(tied(sums, terms)[6])
    one = ring(sent, AHEAD)
    sent = coded(sums[4] + decoded(tied(four, sent)) + decoded(three))
    two = ring(sent, AHEAD_TWO)
    sent = coded(sums[3] + decoded(tied(five, sent)))
    six = ring(sent, BACK_TWO)
    sent = coded(tied(sums, sent)[5])
    seven = ring(sent, BACK)
    terms = tied(terms, sent).reshape(NV, 1, per_device * heads)
    terms = lax.all_to_all(terms, "vocab", 0, 0, axis_index_groups=CORE_MAJOR, tiled=True)
    logits = sums[7] + decoded(one) + decoded(two) + decoded(six) + decoded(seven)

    message = stats(place, logits, terms)
    messages = lax.all_to_all(message, "vocab", 0, 0, tiled=True)
    log_probs, attribution = finish(place, logits, messages, heads, per_device)
    return (log_probs, attribution.T)


def solution(mesh):
    in_specs = (P("vocab", "head", None), P("head", None, "vocab"), P())
    out_specs = (P("head", "vocab"), P(None, "head"))
    return jax.shard_map(
        on_device, mesh=mesh, in_specs=in_specs, out_specs=out_specs, check_vma=False
    )
```

```python
import functools

import jax
import jax.numpy as jnp
from jax import lax
from jax.experimental import pallas as pl
from jax.experimental.pallas import tpu as pltpu
from jax.sharding import PartitionSpec as P

NX, NY, NC, NZ = 4, 8, 2, 8
NV = NX * NY * NC
SCALE = 0.125
MIB = 2**20
SLOT_OF = {4: 0, 5: 1, 3: 2, 6: 3, 2: 4, 7: 5, 1: 6, 0: 7}


def vocab_index(x, y, c):
    return (x * NY + y) * NC + c


Y_GROUPS = [[vocab_index(x, y, c) for y in range(NY)] for x in range(NX) for c in range(NC)]
X_GROUPS = [[vocab_index(x, y, c) for x in range(NX)] for y in range(NY) for c in range(NC)]
CORE_MAJOR = [[vocab_index(x, y, c) for c in range(NC) for x in range(NX) for y in range(NY)]]
CORE_SWAP = [(v, v ^ 1) for v in range(NV)]


def hop(sign):
    pairs = []
    for z in range(NZ):
        for v in range(NV):
            step = sign if v % NC == 0 else -sign
            pairs.append((z * NV + v, (z + step) % NZ * NV + v))
    return pairs


AHEAD, BACK, AHEAD_TWO, BACK_TWO = hop(1), hop(-1), hop(2), hop(-2)


def share(block, groups, count):
    copies = jnp.broadcast_to(block[None], (count,) + block.shape)
    return lax.all_to_all(copies, "vocab", 0, 0, axis_index_groups=groups, tiled=True)


def coded(values):
    return (values * SCALE).astype(jnp.float16)


def decoded(values):
    return values.astype(jnp.float32) * (1.0 / SCALE)


def ring(values, pairs):
    return lax.ppermute(values, ("head", "vocab"), pairs)


def tied(value, earlier):
    return lax.optimization_barrier((value, earlier))[0]


def cost(flops, mib):
    return pl.CostEstimate(flops=flops, bytes_accessed=mib * MIB, transcendentals=0)


def params():
    return pltpu.CompilerParams(vmem_limit_bytes=20 * MIB)


SMEM = pl.BlockSpec(memory_space=pltpu.SMEM)
VMEM = pl.BlockSpec(memory_space=pltpu.VMEM)


def pick_kernel(per_device, place_ref, ids_ref, weights_ref, own_ref, other_ref):
    tokens, slab = ids_ref.shape[0], weights_ref.shape[1]
    core = place_ref[1]
    lanes = lax.broadcasted_iota(jnp.int32, (tokens, slab), 1)
    chosen = (ids_ref[...] == lanes).astype(jnp.float32).astype(jnp.bfloat16)
    picked = lax.dot_general(
        chosen, weights_ref[...], (((1,), (1,)), ((), ())), preferred_element_type=jnp.float32
    ).astype(jnp.bfloat16)
    for place in range(tokens // per_device // NC):
        first = picked[2 * place * per_device : (2 * place + 1) * per_device]
        second = picked[(2 * place + 1) * per_device : (2 * place + 2) * per_device]
        rows = slice(place * per_device, (place + 1) * per_device)
        own_ref[rows] = jnp.where(core == 0, first, second)
        other_ref[rows] = jnp.where(core == 0, second, first)


def pick_columns(place, ids, weights, per_device):
    depth, slab = weights.shape
    tokens = ids.shape[0]
    block = 256
    half = jax.ShapeDtypeStruct((tokens // NC, depth), jnp.bfloat16)
    return pl.pallas_call(
        functools.partial(pick_kernel, per_device),
        grid=(tokens // block,),
        in_specs=[
            SMEM,
            pl.BlockSpec((block, 1), lambda i: (i, 0)),
            pl.BlockSpec((depth, slab), lambda i: (0, 0)),
        ],
        out_specs=[pl.BlockSpec((block // NC, depth), lambda i: (i, 0))] * 2,
        out_shape=[half, half],
        cost_estimate=cost(2 * tokens * depth * slab, 8),
        compiler_params=params(),
    )(place, ids, weights)


def sums_kernel(kind, place_ref, rows_ref, weights_ref, *rest):
    sums_ref = rest[-1]
    z, way = place_ref[0], place_ref[2]
    block = sums_ref.shape[2]
    parts = rows_ref.shape[0] // block
    sums = jnp.dot(rows_ref[...], weights_ref[...], preferred_element_type=jnp.float32)
    for part in range(parts):
        target = pl.program_id(0) * parts + part
        distance = jnp.bitwise_and((target - z) * way, NZ - 1)
        slot = jnp.int32(0)
        for key, value in SLOT_OF.items():
            slot = jnp.where(distance == key, value, slot)
        sums_ref[slot, kind] = sums[part * block : (part + 1) * block]


def partial_sums(place, rows, weights, earlier=None):
    tokens, depth = rows.shape
    slab = weights.shape[1]
    steps = 2
    kind = 0 if earlier is None else 1
    return pl.pallas_call(
        functools.partial(sums_kernel, kind),
        grid=(steps,),
        in_specs=[SMEM, pl.BlockSpec((tokens // steps, depth), lambda i: (i, 0)), VMEM] + [VMEM] * kind,
        out_specs=VMEM,
        out_shape=jax.ShapeDtypeStruct((NZ, NC, tokens // NZ, slab), jnp.float32),
        input_output_aliases={3: 0} if kind else {},
        cost_estimate=cost(2 * tokens * depth * slab, 6),
        compiler_params=params(),
    )(place, rows, weights, *([earlier] if kind else []))


def terms_kernel(heads, per_device, place_ref, own_ref, other_ref, picked_own_ref, picked_other_ref, terms_ref):
    core = place_ref[1]
    tokens, depth = own_ref.shape
    lanes = heads * per_device
    places = tokens // per_device
    head_of = lax.broadcasted_iota(jnp.int32, (depth, lanes), 0) // (depth // heads)
    lane_head = lax.broadcasted_iota(jnp.int32, (depth, lanes), 1) % heads
    spread = (head_of == lane_head).astype(jnp.float32).astype(jnp.bfloat16)
    token = lax.broadcasted_iota(jnp.int32, (places, per_device, lanes), 1)
    lane_token = lax.broadcasted_iota(jnp.int32, (places, per_device, lanes), 2) // heads
    parts = []
    for rows_ref, picked_ref in ((own_ref, picked_own_ref), (other_ref, picked_other_ref)):
        products = rows_ref[...].astype(jnp.float32) * picked_ref[...].astype(jnp.float32)
        high = products.astype(jnp.bfloat16)
        parts += [high, (products - high.astype(jnp.float32)).astype(jnp.bfloat16)]
    sums = jnp.dot(jnp.concatenate(parts, axis=0), spread, preferred_element_type=jnp.float32)
    for kind in range(NC):
        start = 2 * kind * tokens
        terms = sums[start : start + tokens] + sums[start + tokens : start + 2 * tokens]
        terms = jnp.where(token == lane_token, terms.reshape(places, per_device, lanes), 0.0)
        terms_ref[jnp.bitwise_xor(core, kind), :, 0] = jnp.sum(terms, axis=1)


def head_terms(place, own, other, picked_own, picked_other, heads, per_device):
    tokens, depth = own.shape
    lanes = heads * per_device
    steps = 2
    rows = pl.BlockSpec((tokens // steps, depth), lambda i: (i, 0))
    places = tokens // per_device
    return pl.pallas_call(
        functools.partial(terms_kernel, heads, per_device),
        grid=(steps,),
        in_specs=[SMEM, rows, rows, rows, rows],
        out_specs=pl.BlockSpec((NC, places // steps, 1, lanes), lambda i: (0, i, 0, 0)),
        out_shape=jax.ShapeDtypeStruct((NC, places, 1, lanes), jnp.float32),
        cost_estimate=cost(16 * tokens * depth * lanes, 4),
        compiler_params=params(),
    )(place, own, other, picked_own, picked_other)


def eye(size):
    rows = lax.broadcasted_iota(jnp.int32, (size, size), 0)
    return rows == lax.broadcasted_iota(jnp.int32, (size, size), 1)


def stats_kernel(place_ref, logits_ref, terms_ref, message_ref):
    core = place_ref[1]
    found = []
    for kind in range(NC):
        logits = logits_ref[kind]
        top = jnp.max(logits, axis=1, keepdims=True)
        found.append(top + jnp.log(jnp.sum(jnp.exp(logits - top), axis=1, keepdims=True)))
    own, other = found
    lse = jnp.concatenate([jnp.where(core == 0, own, other), jnp.where(core == 0, other, own)], axis=0)
    size = lse.shape[0]
    lse = jnp.sum(jnp.where(eye(size), lse, 0.0), axis=0, keepdims=True)
    terms = jnp.sum(terms_ref[...], axis=0)
    message = jnp.concatenate([lse, terms], axis=0)
    message_ref[...] = jnp.broadcast_to(message[None], message_ref.shape)


def stats(place, logits, terms):
    size = NC * logits.shape[1]
    return pl.pallas_call(
        stats_kernel,
        in_specs=[SMEM, VMEM, VMEM],
        out_specs=VMEM,
        out_shape=jax.ShapeDtypeStruct((NV, 2, size), jnp.float32),
        cost_estimate=cost(0, 1),
        compiler_params=params(),
    )(place, logits, terms)


def finish_kernel(heads, per_device, place_ref, logits_ref, messages_ref, out_ref, attribution_ref):
    core = place_ref[1]
    every = messages_ref[:, 0, :]
    size = every.shape[1]
    top = jnp.max(every, axis=0, keepdims=True)
    lse = top + jnp.log(jnp.sum(jnp.exp(every - top), axis=0, keepdims=True))
    lse = jnp.sum(jnp.where(eye(size), lse, 0.0), axis=1, keepdims=True)
    half = size // NC
    for c in range(NC):
        logits = logits_ref[jnp.bitwise_xor(core, c)]
        values = (logits - lse[c * half : (c + 1) * half]).astype(out_ref.dtype)
        for place in range(half // per_device):
            start = (place * NC + c) * per_device
            out_ref[start : start + per_device] = values[place * per_device : (place + 1) * per_device]
    terms = messages_ref[:, 1, :]
    shape = (NV, per_device, size)
    token = lax.broadcasted_iota(jnp.int32, shape, 1)
    lane_token = lax.broadcasted_iota(jnp.int32, shape, 2) // heads
    terms = jnp.where(token == lane_token, jnp.broadcast_to(terms[:, None, :], shape), 0.0)
    head = lax.broadcasted_iota(jnp.int32, (heads, size), 0)
    lane_head = lax.broadcasted_iota(jnp.int32, (heads, size), 1) % heads
    attribution_ref[...] = lax.dot_general(
        (head == lane_head).astype(jnp.float32),
        terms.reshape(NV * per_device, size),
        (((1,), (1,)), ((), ())),
        preferred_element_type=jnp.float32,
        precision=lax.Precision.HIGHEST,
    )


def finish(place, logits, messages, heads, per_device):
    tokens, slab = NC * logits.shape[1], logits.shape[2]
    return pl.pallas_call(
        functools.partial(finish_kernel, heads, per_device),
        in_specs=[SMEM, VMEM, VMEM],
        out_specs=[VMEM, VMEM],
        out_shape=[
            jax.ShapeDtypeStruct((tokens, slab), jnp.bfloat16),
            jax.ShapeDtypeStruct((heads, NV * per_device), jnp.float32),
        ],
        cost_estimate=cost(0, 1),
        compiler_params=params(),
    )(place, logits, messages)


def on_device(heads_out, unembed, targets):
    per_device, heads, hd = heads_out.shape
    depth = heads * hd
    slab = unembed.shape[2]
    weights = unembed.reshape(depth, slab)
    vocab_id = lax.axis_index("vocab")
    z = lax.axis_index("head")
    core = vocab_id & 1
    way = 1 - 2 * core
    place = jnp.stack([z, core, way])
    ids = (targets - vocab_id * slab).reshape(-1, 1)
    picked_own, picked_other = pick_columns(place, ids, weights, per_device)
    column = share(heads_out.reshape(per_device, depth), Y_GROUPS, NY)
    own = share(column, X_GROUPS, NX).reshape(-1, depth)
    own = tied(own, picked_own)
    other = lax.ppermute(own, "vocab", CORE_SWAP)
    sums = partial_sums(place, own, weights)
    sums = partial_sums(place, tied(other, sums), weights, sums)

    sent = coded(sums[0])
    four = ring(sent, AHEAD_TWO)
    sent = coded(tied(sums, sent)[2])
    three = ring(sent, AHEAD)
    sent = coded(tied(sums, sent)[1])
    five = ring(sent, BACK)
    sent = coded(tied(sums, sent)[6])
    one = ring(sent, AHEAD)
    terms = head_terms(place, own, tied(other, sent), picked_own, picked_other, heads, per_device)
    sums = tied(sums, terms)
    sent = coded(tied(sums, sent)[5])
    seven = ring(sent, BACK)
    sent = coded(sums[4] + decoded(tied(four, sent)) + decoded(three))
    two = ring(sent, AHEAD_TWO)
    sent = coded(sums[3] + decoded(tied(five, sent)))
    six = ring(sent, BACK_TWO)
    terms = tied(terms, sent).reshape(NV, 1, per_device * heads)
    terms = lax.all_to_all(terms, "vocab", 0, 0, axis_index_groups=CORE_MAJOR, tiled=True)
    part = tied(sums, sent)[7] + decoded(one) + decoded(seven)
    sent = tied(sent, part)
    logits = part + decoded(two) + decoded(six)

    message = stats(place, logits, terms)
    messages = lax.all_to_all(message, "vocab", 0, 0, tiled=True)
    log_probs, attribution = finish(place, logits, messages, heads, per_device)
    return (log_probs, attribution.T)


def solution(mesh):
    in_specs = (P("vocab", "head", None), P("head", None, "vocab"), P())
    out_specs = (P("head", "vocab"), P(None, "head"))
    return jax.shard_map(
        on_device, mesh=mesh, in_specs=in_specs, out_specs=out_specs, check_vma=False
    )
```

```python
import functools

import jax
import jax.numpy as jnp
from jax import lax
from jax.experimental import pallas as pl
from jax.experimental.pallas import tpu as pltpu
from jax.sharding import PartitionSpec as P

NX, NY, NC, NZ = 4, 8, 2, 8
NV = NX * NY * NC
SCALE = 0.125
MIB = 2**20
SLOT_OF = {4: 0, 5: 1, 3: 2, 6: 3, 2: 4, 7: 5, 1: 6, 0: 7}


def vocab_index(x, y, c):
    return (x * NY + y) * NC + c


Y_GROUPS = [[vocab_index(x, y, c) for y in range(NY)] for x in range(NX) for c in range(NC)]
X_GROUPS = [[vocab_index(x, y, c) for x in range(NX)] for y in range(NY) for c in range(NC)]
CORE_MAJOR = [[vocab_index(x, y, c) for c in range(NC) for x in range(NX) for y in range(NY)]]
CORE_SWAP = [(v, v ^ 1) for v in range(NV)]


def hop(sign):
    pairs = []
    for z in range(NZ):
        for v in range(NV):
            step = sign if v % NC == 0 else -sign
            pairs.append((z * NV + v, (z + step) % NZ * NV + v))
    return pairs


AHEAD, BACK, AHEAD_TWO, BACK_TWO = hop(1), hop(-1), hop(2), hop(-2)


def share(block, groups, count):
    copies = jnp.broadcast_to(block[None], (count,) + block.shape)
    return lax.all_to_all(copies, "vocab", 0, 0, axis_index_groups=groups, tiled=True)


def coded(values):
    return (values * SCALE).astype(jnp.float16)


def decoded(values):
    return values.astype(jnp.float32) * (1.0 / SCALE)


def ring(values, pairs):
    return lax.ppermute(values, ("head", "vocab"), pairs)


def tied(value, earlier):
    return lax.optimization_barrier((value, earlier))[0]


def cost(flops, mib):
    return pl.CostEstimate(flops=flops, bytes_accessed=mib * MIB, transcendentals=0)


def params():
    return pltpu.CompilerParams(vmem_limit_bytes=20 * MIB)


SMEM = pl.BlockSpec(memory_space=pltpu.SMEM)
VMEM = pl.BlockSpec(memory_space=pltpu.VMEM)


def pick_kernel(per_device, place_ref, ids_ref, weights_ref, own_ref, other_ref):
    tokens, slab = ids_ref.shape[0], weights_ref.shape[1]
    core = place_ref[1]
    lanes = lax.broadcasted_iota(jnp.int32, (tokens, slab), 1)
    chosen = (ids_ref[...] == lanes).astype(jnp.float32).astype(jnp.bfloat16)
    picked = lax.dot_general(
        chosen, weights_ref[...], (((1,), (1,)), ((), ())), preferred_element_type=jnp.float32
    ).astype(jnp.bfloat16)
    for place in range(tokens // per_device // NC):
        first = picked[2 * place * per_device : (2 * place + 1) * per_device]
        second = picked[(2 * place + 1) * per_device : (2 * place + 2) * per_device]
        rows = slice(place * per_device, (place + 1) * per_device)
        own_ref[rows] = jnp.where(core == 0, first, second)
        other_ref[rows] = jnp.where(core == 0, second, first)


def pick_columns(place, ids, weights, per_device):
    depth, slab = weights.shape
    tokens = ids.shape[0]
    block = 256
    half = jax.ShapeDtypeStruct((tokens // NC, depth), jnp.bfloat16)
    return pl.pallas_call(
        functools.partial(pick_kernel, per_device),
        grid=(tokens // block,),
        in_specs=[
            SMEM,
            pl.BlockSpec((block, 1), lambda i: (i, 0)),
            pl.BlockSpec((depth, slab), lambda i: (0, 0)),
        ],
        out_specs=[pl.BlockSpec((block // NC, depth), lambda i: (i, 0))] * 2,
        out_shape=[half, half],
        cost_estimate=cost(2 * tokens * depth * slab, 8),
        compiler_params=params(),
    )(place, ids, weights)


def sums_kernel(kind, place_ref, rows_ref, weights_ref, *rest):
    sums_ref = rest[-1]
    z, way = place_ref[0], place_ref[2]
    block = sums_ref.shape[2]
    parts = rows_ref.shape[0] // block
    sums = jnp.dot(rows_ref[...], weights_ref[...], preferred_element_type=jnp.float32)
    for part in range(parts):
        target = pl.program_id(0) * parts + part
        distance = jnp.bitwise_and((target - z) * way, NZ - 1)
        slot = jnp.int32(0)
        for key, value in SLOT_OF.items():
            slot = jnp.where(distance == key, value, slot)
        sums_ref[slot, kind] = sums[part * block : (part + 1) * block]


def partial_sums(place, rows, weights, earlier=None):
    tokens, depth = rows.shape
    slab = weights.shape[1]
    steps = 2
    kind = 0 if earlier is None else 1
    return pl.pallas_call(
        functools.partial(sums_kernel, kind),
        grid=(steps,),
        in_specs=[SMEM, pl.BlockSpec((tokens // steps, depth), lambda i: (i, 0)), VMEM] + [VMEM] * kind,
        out_specs=VMEM,
        out_shape=jax.ShapeDtypeStruct((NZ, NC, tokens // NZ, slab), jnp.float32),
        input_output_aliases={3: 0} if kind else {},
        cost_estimate=cost(2 * tokens * depth * slab, 6),
        compiler_params=params(),
    )(place, rows, weights, *([earlier] if kind else []))


def terms_kernel(heads, per_device, place_ref, own_ref, other_ref, picked_own_ref, picked_other_ref, terms_ref):
    core = place_ref[1]
    tokens, depth = own_ref.shape
    lanes = heads * per_device
    places = tokens // per_device
    head_of = lax.broadcasted_iota(jnp.int32, (depth, lanes), 0) // (depth // heads)
    lane_head = lax.broadcasted_iota(jnp.int32, (depth, lanes), 1) % heads
    spread = (head_of == lane_head).astype(jnp.float32).astype(jnp.bfloat16)
    token = lax.broadcasted_iota(jnp.int32, (places, per_device, lanes), 1)
    lane_token = lax.broadcasted_iota(jnp.int32, (places, per_device, lanes), 2) // heads
    parts = []
    for rows_ref, picked_ref in ((own_ref, picked_own_ref), (other_ref, picked_other_ref)):
        products = rows_ref[...].astype(jnp.float32) * picked_ref[...].astype(jnp.float32)
        high = products.astype(jnp.bfloat16)
        parts += [high, (products - high.astype(jnp.float32)).astype(jnp.bfloat16)]
    sums = jnp.dot(jnp.concatenate(parts, axis=0), spread, preferred_element_type=jnp.float32)
    for kind in range(NC):
        start = 2 * kind * tokens
        terms = sums[start : start + tokens] + sums[start + tokens : start + 2 * tokens]
        terms = jnp.where(token == lane_token, terms.reshape(places, per_device, lanes), 0.0)
        terms_ref[jnp.bitwise_xor(core, kind), :, 0] = jnp.sum(terms, axis=1)


def head_terms(place, own, other, picked_own, picked_other, heads, per_device):
    tokens, depth = own.shape
    lanes = heads * per_device
    steps = 2
    rows = pl.BlockSpec((tokens // steps, depth), lambda i: (i, 0))
    places = tokens // per_device
    return pl.pallas_call(
        functools.partial(terms_kernel, heads, per_device),
        grid=(steps,),
        in_specs=[SMEM, rows, rows, rows, rows],
        out_specs=pl.BlockSpec((NC, places // steps, 1, lanes), lambda i: (0, i, 0, 0)),
        out_shape=jax.ShapeDtypeStruct((NC, places, 1, lanes), jnp.float32),
        cost_estimate=cost(16 * tokens * depth * lanes, 4),
        compiler_params=params(),
    )(place, own, other, picked_own, picked_other)


def eye(size):
    rows = lax.broadcasted_iota(jnp.int32, (size, size), 0)
    return rows == lax.broadcasted_iota(jnp.int32, (size, size), 1)


def stats_kernel(place_ref, logits_ref, terms_ref, message_ref):
    core = place_ref[1]
    found = []
    for kind in range(NC):
        logits = logits_ref[kind]
        top = jnp.max(logits, axis=1, keepdims=True)
        found.append(top + jnp.log(jnp.sum(jnp.exp(logits - top), axis=1, keepdims=True)))
    own, other = found
    lse = jnp.concatenate([jnp.where(core == 0, own, other), jnp.where(core == 0, other, own)], axis=0)
    size = lse.shape[0]
    lse = jnp.sum(jnp.where(eye(size), lse, 0.0), axis=0, keepdims=True)
    terms = jnp.sum(terms_ref[...], axis=0)
    message = jnp.concatenate([lse, terms], axis=0)
    message_ref[...] = jnp.broadcast_to(message[None], message_ref.shape)


def stats(place, logits, terms):
    size = NC * logits.shape[1]
    return pl.pallas_call(
        stats_kernel,
        in_specs=[SMEM, VMEM, VMEM],
        out_specs=VMEM,
        out_shape=jax.ShapeDtypeStruct((NV, 2, size), jnp.float32),
        cost_estimate=cost(0, 1),
        compiler_params=params(),
    )(place, logits, terms)


def finish_kernel(heads, per_device, place_ref, logits_ref, messages_ref, out_ref, attribution_ref):
    core = place_ref[1]
    every = messages_ref[:, 0, :]
    size = every.shape[1]
    top = jnp.max(every, axis=0, keepdims=True)
    lse = top + jnp.log(jnp.sum(jnp.exp(every - top), axis=0, keepdims=True))
    lse = jnp.sum(jnp.where(eye(size), lse, 0.0), axis=1, keepdims=True)
    half = size // NC
    for c in range(NC):
        logits = logits_ref[jnp.bitwise_xor(core, c)]
        values = (logits - lse[c * half : (c + 1) * half]).astype(out_ref.dtype)
        for place in range(half // per_device):
            start = (place * NC + c) * per_device
            out_ref[start : start + per_device] = values[place * per_device : (place + 1) * per_device]
    shape = (NV, per_device, size)
    token = lax.broadcasted_iota(jnp.int32, shape, 1)
    here = token == lax.broadcasted_iota(jnp.int32, shape, 2) // heads
    head = lax.broadcasted_iota(jnp.int32, (heads, size), 0)
    lane_head = lax.broadcasted_iota(jnp.int32, (heads, size), 1) % heads
    same = (head == lane_head).astype(jnp.float32).astype(jnp.bfloat16)
    left = messages_ref[:, 1, :]
    total = jnp.zeros((heads, NV * per_device), jnp.float32)
    for _ in range(3):
        part = left.astype(jnp.bfloat16).astype(jnp.float32)
        left = left - part
        spread = jnp.where(here, jnp.broadcast_to(part[:, None, :], shape), 0.0)
        spread = spread.reshape(NV * per_device, size).astype(jnp.bfloat16)
        total += lax.dot_general(same, spread, (((1,), (1,)), ((), ())), preferred_element_type=jnp.float32)
    attribution_ref[...] = total


def finish(place, logits, messages, heads, per_device):
    tokens, slab = NC * logits.shape[1], logits.shape[2]
    return pl.pallas_call(
        functools.partial(finish_kernel, heads, per_device),
        in_specs=[SMEM, VMEM, VMEM],
        out_specs=[VMEM, VMEM],
        out_shape=[
            jax.ShapeDtypeStruct((tokens, slab), jnp.bfloat16),
            jax.ShapeDtypeStruct((heads, NV * per_device), jnp.float32),
        ],
        cost_estimate=cost(0, 1),
        compiler_params=params(),
    )(place, logits, messages)


def on_device(heads_out, unembed, targets):
    per_device, heads, hd = heads_out.shape
    depth = heads * hd
    slab = unembed.shape[2]
    weights = unembed.reshape(depth, slab)
    vocab_id = lax.axis_index("vocab")
    z = lax.axis_index("head")
    core = vocab_id & 1
    way = 1 - 2 * core
    place = jnp.stack([z, core, way])
    ids = (targets - vocab_id * slab).reshape(-1, 1)
    picked_own, picked_other = pick_columns(place, ids, weights, per_device)
    column = share(heads_out.reshape(per_device, depth), Y_GROUPS, NY)
    own = share(column, X_GROUPS, NX).reshape(-1, depth)
    own = tied(own, picked_own)
    other = lax.ppermute(own, "vocab", CORE_SWAP)
    sums = partial_sums(place, own, weights)
    sums = partial_sums(place, tied(other, sums), weights, sums)

    sent = coded(sums[0])
    four = ring(sent, AHEAD_TWO)
    sent = coded(tied(sums, sent)[2])
    three = ring(sent, AHEAD)
    sent = coded(tied(sums, sent)[1])
    five = ring(sent, BACK)
    sent = coded(tied(sums, sent)[6])
    one = ring(sent, AHEAD)
    terms = head_terms(place, own, tied(other, sent), picked_own, picked_other, heads, per_device)
    sums = tied(sums, terms)
    sent = coded(tied(sums, sent)[5])
    seven = ring(sent, BACK)
    sent = coded(sums[3] + decoded(tied(five, sent)))
    six = ring(sent, BACK_TWO)
    sent = coded(sums[4] + decoded(tied(four, sent)) + decoded(three))
    two = ring(sent, AHEAD_TWO)
    terms = tied(terms, sent).reshape(NV, 1, per_device * heads)
    terms = lax.all_to_all(terms, "vocab", 0, 0, axis_index_groups=CORE_MAJOR, tiled=True)
    part = tied(sums, sent)[7] + decoded(one) + decoded(seven)
    logits = tied(part, sent) + decoded(two) + decoded(six)

    message = stats(place, logits, terms)
    messages = lax.all_to_all(message, "vocab", 0, 0, tiled=True)
    log_probs, attribution = finish(place, logits, messages, heads, per_device)
    return (log_probs, attribution.T)


def solution(mesh):
    in_specs = (P("vocab", "head", None), P("head", None, "vocab"), P())
    out_specs = (P("head", "vocab"), P(None, "head"))
    return jax.shard_map(
        on_device, mesh=mesh, in_specs=in_specs, out_specs=out_specs, check_vma=False
    )
```

```python
import functools

import jax
import jax.numpy as jnp
from jax import lax
from jax.experimental import pallas as pl
from jax.experimental.pallas import tpu as pltpu
from jax.sharding import PartitionSpec as P

NX, NY, NC, NZ = 4, 8, 2, 8
NV = NX * NY * NC
SCALE = 0.125
MIB = 2**20
SLOT_OF = {4: 0, 5: 1, 3: 2, 6: 3, 2: 4, 7: 5, 1: 6, 0: 7}


def vocab_index(x, y, c):
    return (x * NY + y) * NC + c


Y_GROUPS = [[vocab_index(x, y, c) for y in range(NY)] for x in range(NX) for c in range(NC)]
X_GROUPS = [[vocab_index(x, y, c) for x in range(NX)] for y in range(NY) for c in range(NC)]
CORE_MAJOR = [[vocab_index(x, y, c) for c in range(NC) for x in range(NX) for y in range(NY)]]
CORE_SWAP = [(v, v ^ 1) for v in range(NV)]


def hop(sign):
    pairs = []
    for z in range(NZ):
        for v in range(NV):
            step = sign if v % NC == 0 else -sign
            pairs.append((z * NV + v, (z + step) % NZ * NV + v))
    return pairs


AHEAD, BACK, AHEAD_TWO, BACK_TWO = hop(1), hop(-1), hop(2), hop(-2)


def share(block, groups, count):
    copies = jnp.broadcast_to(block[None], (count,) + block.shape)
    return lax.all_to_all(copies, "vocab", 0, 0, axis_index_groups=groups, tiled=True)


def coded(values):
    return (values * SCALE).astype(jnp.float16)


def decoded(values):
    return values.astype(jnp.float32) * (1.0 / SCALE)


def ring(values, pairs):
    return lax.ppermute(values, ("head", "vocab"), pairs)


def tied(value, earlier):
    return lax.optimization_barrier((value, earlier))[0]


def cost(flops, mib):
    return pl.CostEstimate(flops=flops, bytes_accessed=mib * MIB, transcendentals=0)


def params():
    return pltpu.CompilerParams(vmem_limit_bytes=14 * MIB)


SMEM = pl.BlockSpec(memory_space=pltpu.SMEM)
VMEM = pl.BlockSpec(memory_space=pltpu.VMEM)


def pick_kernel(per_device, place_ref, ids_ref, weights_ref, own_ref, other_ref):
    tokens, slab = ids_ref.shape[0], weights_ref.shape[1]
    core = place_ref[1]
    lanes = lax.broadcasted_iota(jnp.int32, (tokens, slab), 1)
    chosen = (ids_ref[...] == lanes).astype(jnp.float32).astype(jnp.bfloat16)
    picked = lax.dot_general(
        chosen, weights_ref[...], (((1,), (1,)), ((), ())), preferred_element_type=jnp.float32
    ).astype(jnp.bfloat16)
    for place in range(tokens // per_device // NC):
        first = picked[2 * place * per_device : (2 * place + 1) * per_device]
        second = picked[(2 * place + 1) * per_device : (2 * place + 2) * per_device]
        rows = slice(place * per_device, (place + 1) * per_device)
        own_ref[rows] = jnp.where(core == 0, first, second)
        other_ref[rows] = jnp.where(core == 0, second, first)


def pick_columns(place, ids, weights, per_device):
    depth, slab = weights.shape
    tokens = ids.shape[0]
    block = 256
    half = jax.ShapeDtypeStruct((tokens // NC, depth), jnp.bfloat16)
    return pl.pallas_call(
        functools.partial(pick_kernel, per_device),
        grid=(tokens // block,),
        in_specs=[
            SMEM,
            pl.BlockSpec((block, 1), lambda i: (i, 0)),
            pl.BlockSpec((depth, slab), lambda i: (0, 0)),
        ],
        out_specs=[pl.BlockSpec((block // NC, depth), lambda i: (i, 0))] * 2,
        out_shape=[half, half],
        cost_estimate=cost(2 * tokens * depth * slab, 8),
        compiler_params=params(),
    )(place, ids, weights)


def sums_kernel(kind, place_ref, rows_ref, weights_ref, *rest):
    sums_ref = rest[-1]
    z, way = place_ref[0], place_ref[2]
    block = sums_ref.shape[2]
    parts = rows_ref.shape[0] // block
    sums = jnp.dot(rows_ref[...], weights_ref[...], preferred_element_type=jnp.float32)
    for part in range(parts):
        distance = jnp.bitwise_and((part - z) * way, NZ - 1)
        slot = jnp.int32(0)
        for key, value in SLOT_OF.items():
            slot = jnp.where(distance == key, value, slot)
        sums_ref[slot, kind] = sums[part * block : (part + 1) * block]


def partial_sums(place, rows, weights, earlier=None):
    tokens, depth = rows.shape
    slab = weights.shape[1]
    kind = 0 if earlier is None else 1
    return pl.pallas_call(
        functools.partial(sums_kernel, kind),
        in_specs=[SMEM, VMEM, VMEM] + [VMEM] * kind,
        out_specs=VMEM,
        out_shape=jax.ShapeDtypeStruct((NZ, NC, tokens // NZ, slab), jnp.float32),
        input_output_aliases={3: 0} if kind else {},
        cost_estimate=cost(2 * tokens * depth * slab, 6),
        compiler_params=params(),
    )(place, rows, weights, *([earlier] if kind else []))


def terms_kernel(heads, per_device, place_ref, own_ref, other_ref, picked_own_ref, picked_other_ref, terms_ref):
    core = place_ref[1]
    tokens, depth = own_ref.shape
    lanes = heads * per_device
    places = tokens // per_device
    head_of = lax.broadcasted_iota(jnp.int32, (depth, lanes), 0) // (depth // heads)
    lane_head = lax.broadcasted_iota(jnp.int32, (depth, lanes), 1) % heads
    spread = (head_of == lane_head).astype(jnp.float32).astype(jnp.bfloat16)
    token = lax.broadcasted_iota(jnp.int32, (places, per_device, lanes), 1)
    lane_token = lax.broadcasted_iota(jnp.int32, (places, per_device, lanes), 2) // heads
    parts = []
    for rows_ref, picked_ref in ((own_ref, picked_own_ref), (other_ref, picked_other_ref)):
        products = rows_ref[...].astype(jnp.float32) * picked_ref[...].astype(jnp.float32)
        high = products.astype(jnp.bfloat16)
        parts += [high, (products - high.astype(jnp.float32)).astype(jnp.bfloat16)]
    sums = jnp.dot(jnp.concatenate(parts, axis=0), spread, preferred_element_type=jnp.float32)
    for kind in range(NC):
        start = 2 * kind * tokens
        terms = sums[start : start + tokens] + sums[start + tokens : start + 2 * tokens]
        terms = jnp.where(token == lane_token, terms.reshape(places, per_device, lanes), 0.0)
        terms_ref[jnp.bitwise_xor(core, kind), :, 0] = jnp.sum(terms, axis=1)


def head_terms(place, own, other, picked_own, picked_other, heads, per_device):
    tokens, depth = own.shape
    lanes = heads * per_device
    steps = 2
    rows = pl.BlockSpec((tokens // steps, depth), lambda i: (i, 0))
    places = tokens // per_device
    return pl.pallas_call(
        functools.partial(terms_kernel, heads, per_device),
        grid=(steps,),
        in_specs=[SMEM, rows, rows, rows, rows],
        out_specs=pl.BlockSpec((NC, places // steps, 1, lanes), lambda i: (0, i, 0, 0)),
        out_shape=jax.ShapeDtypeStruct((NC, places, 1, lanes), jnp.float32),
        cost_estimate=cost(16 * tokens * depth * lanes, 4),
        compiler_params=params(),
    )(place, own, other, picked_own, picked_other)


def eye(size):
    rows = lax.broadcasted_iota(jnp.int32, (size, size), 0)
    return rows == lax.broadcasted_iota(jnp.int32, (size, size), 1)


def stats_kernel(place_ref, logits_ref, terms_ref, message_ref):
    core = place_ref[1]
    found = []
    for kind in range(NC):
        logits = logits_ref[kind]
        top = jnp.max(logits, axis=1, keepdims=True)
        found.append(top + jnp.log(jnp.sum(jnp.exp(logits - top), axis=1, keepdims=True)))
    own, other = found
    lse = jnp.concatenate([jnp.where(core == 0, own, other), jnp.where(core == 0, other, own)], axis=0)
    size = lse.shape[0]
    lse = jnp.sum(jnp.where(eye(size), lse, 0.0), axis=0, keepdims=True)
    terms = jnp.sum(terms_ref[...], axis=0)
    message = jnp.concatenate([lse, terms], axis=0)
    message_ref[...] = jnp.broadcast_to(message[None], message_ref.shape)


def stats(place, logits, terms):
    size = NC * logits.shape[1]
    return pl.pallas_call(
        stats_kernel,
        in_specs=[SMEM, VMEM, VMEM],
        out_specs=VMEM,
        out_shape=jax.ShapeDtypeStruct((NV, 2, size), jnp.float32),
        cost_estimate=cost(0, 1),
        compiler_params=params(),
    )(place, logits, terms)


def finish_kernel(heads, per_device, place_ref, logits_ref, messages_ref, out_ref, attribution_ref):
    core = place_ref[1]
    every = messages_ref[:, 0, :]
    size = every.shape[1]
    top = jnp.max(every, axis=0, keepdims=True)
    lse = top + jnp.log(jnp.sum(jnp.exp(every - top), axis=0, keepdims=True))
    lse = jnp.sum(jnp.where(eye(size), lse, 0.0), axis=1, keepdims=True)
    half = size // NC
    for c in range(NC):
        logits = logits_ref[jnp.bitwise_xor(core, c)]
        values = (logits - lse[c * half : (c + 1) * half]).astype(out_ref.dtype)
        for place in range(half // per_device):
            start = (place * NC + c) * per_device
            out_ref[start : start + per_device] = values[place * per_device : (place + 1) * per_device]
    shape = (NV, per_device, size)
    token = lax.broadcasted_iota(jnp.int32, shape, 1)
    here = token == lax.broadcasted_iota(jnp.int32, shape, 2) // heads
    head = lax.broadcasted_iota(jnp.int32, (heads, size), 0)
    lane_head = lax.broadcasted_iota(jnp.int32, (heads, size), 1) % heads
    same = (head == lane_head).astype(jnp.float32).astype(jnp.bfloat16)
    left = messages_ref[:, 1, :]
    total = jnp.zeros((heads, NV * per_device), jnp.float32)
    for _ in range(3):
        part = left.astype(jnp.bfloat16).astype(jnp.float32)
        left = left - part
        spread = jnp.where(here, jnp.broadcast_to(part[:, None, :], shape), 0.0)
        spread = spread.reshape(NV * per_device, size).astype(jnp.bfloat16)
        total += lax.dot_general(same, spread, (((1,), (1,)), ((), ())), preferred_element_type=jnp.float32)
    attribution_ref[...] = total


def finish(place, logits, messages, heads, per_device):
    tokens, slab = NC * logits.shape[1], logits.shape[2]
    return pl.pallas_call(
        functools.partial(finish_kernel, heads, per_device),
        in_specs=[SMEM, VMEM, VMEM],
        out_specs=[VMEM, VMEM],
        out_shape=[
            jax.ShapeDtypeStruct((tokens, slab), jnp.bfloat16),
            jax.ShapeDtypeStruct((heads, NV * per_device), jnp.float32),
        ],
        cost_estimate=cost(0, 1),
        compiler_params=params(),
    )(place, logits, messages)


def on_device(heads_out, unembed, targets):
    per_device, heads, hd = heads_out.shape
    depth = heads * hd
    slab = unembed.shape[2]
    weights = unembed.reshape(depth, slab)
    vocab_id = lax.axis_index("vocab")
    z = lax.axis_index("head")
    core = vocab_id & 1
    way = 1 - 2 * core
    place = jnp.stack([z, core, way])
    ids = (targets - vocab_id * slab).reshape(-1, 1)
    picked_own, picked_other = pick_columns(place, ids, weights, per_device)
    column = share(heads_out.reshape(per_device, depth), Y_GROUPS, NY)
    own = share(column, X_GROUPS, NX).reshape(-1, depth)
    own = tied(own, picked_own)
    other = lax.ppermute(own, "vocab", CORE_SWAP)
    sums = partial_sums(place, own, weights)
    sums = partial_sums(place, tied(other, sums), weights, sums)

    sent = coded(sums[0])
    four = ring(sent, AHEAD_TWO)
    sent = coded(tied(sums, sent)[2])
    three = ring(sent, AHEAD)
    sent = coded(tied(sums, sent)[1])
    five = ring(sent, BACK)
    sent = coded(tied(sums, sent)[6])
    one = ring(sent, AHEAD)
    terms = head_terms(place, own, tied(other, sent), picked_own, picked_other, heads, per_device)
    sums = tied(sums, terms)
    sent = coded(tied(sums, sent)[5])
    seven = ring(sent, BACK)
    sent = coded(sums[3] + decoded(tied(five, sent)))
    six = ring(sent, BACK_TWO)
    sent = coded(sums[4] + decoded(tied(four, sent)) + decoded(three))
    two = ring(sent, AHEAD_TWO)
    terms = tied(terms, sent).reshape(NV, 1, per_device * heads)
    terms = lax.all_to_all(terms, "vocab", 0, 0, axis_index_groups=CORE_MAJOR, tiled=True)
    part = tied(sums, sent)[7] + decoded(one) + decoded(seven)
    logits = tied(part, sent) + decoded(two) + decoded(six)

    message = stats(place, logits, terms)
    messages = lax.all_to_all(message, "vocab", 0, 0, tiled=True)
    log_probs, attribution = finish(place, logits, messages, heads, per_device)
    return (log_probs, attribution.T)


def solution(mesh):
    in_specs = (P("vocab", "head", None), P("head", None, "vocab"), P())
    out_specs = (P("head", "vocab"), P(None, "head"))
    return jax.shard_map(
        on_device, mesh=mesh, in_specs=in_specs, out_specs=out_specs, check_vma=False
    )
```

```python
import functools

import jax
import jax.numpy as jnp
from jax import lax
from jax.experimental import pallas as pl
from jax.experimental.pallas import tpu as pltpu
from jax.sharding import PartitionSpec as P

NX, NY, NC, NZ = 4, 8, 2, 8
NV = NX * NY * NC
SCALE = 0.125
MIB = 2**20
SLOT_OF = {4: 0, 5: 1, 3: 2, 6: 3, 2: 4, 7: 5, 1: 6, 0: 7}


def vocab_index(x, y, c):
    return (x * NY + y) * NC + c


Y_GROUPS = [[vocab_index(x, y, c) for y in range(NY)] for x in range(NX) for c in range(NC)]
X_GROUPS = [[vocab_index(x, y, c) for x in range(NX)] for y in range(NY) for c in range(NC)]
CORE_MAJOR = [[vocab_index(x, y, c) for c in range(NC) for x in range(NX) for y in range(NY)]]
CORE_SWAP = [(v, v ^ 1) for v in range(NV)]


def hop(sign):
    pairs = []
    for z in range(NZ):
        for v in range(NV):
            step = sign if v % NC == 0 else -sign
            pairs.append((z * NV + v, (z + step) % NZ * NV + v))
    return pairs


AHEAD, BACK, AHEAD_TWO, BACK_TWO = hop(1), hop(-1), hop(2), hop(-2)


def share(block, groups, count):
    copies = jnp.broadcast_to(block[None], (count,) + block.shape)
    return lax.all_to_all(copies, "vocab", 0, 0, axis_index_groups=groups, tiled=True)


def coded(values):
    return (values * SCALE).astype(jnp.float16)


def decoded(values):
    return values.astype(jnp.float32) * (1.0 / SCALE)


def ring(values, pairs):
    return lax.ppermute(values, ("head", "vocab"), pairs)


def tied(value, earlier):
    return lax.optimization_barrier((value, earlier))[0]


def cost(flops, mib):
    return pl.CostEstimate(flops=flops, bytes_accessed=mib * MIB, transcendentals=0)


def params():
    return pltpu.CompilerParams(vmem_limit_bytes=20 * MIB)


SMEM = pl.BlockSpec(memory_space=pltpu.SMEM)
VMEM = pl.BlockSpec(memory_space=pltpu.VMEM)


def pick_kernel(per_device, place_ref, ids_ref, weights_ref, own_ref, other_ref):
    tokens, slab = ids_ref.shape[0], weights_ref.shape[1]
    core = place_ref[1]
    lanes = lax.broadcasted_iota(jnp.int32, (tokens, slab), 1)
    chosen = (ids_ref[...] == lanes).astype(jnp.float32).astype(jnp.bfloat16)
    picked = lax.dot_general(
        chosen, weights_ref[...], (((1,), (1,)), ((), ())), preferred_element_type=jnp.float32
    ).astype(jnp.bfloat16)
    for place in range(tokens // per_device // NC):
        first = picked[2 * place * per_device : (2 * place + 1) * per_device]
        second = picked[(2 * place + 1) * per_device : (2 * place + 2) * per_device]
        rows = slice(place * per_device, (place + 1) * per_device)
        own_ref[rows] = jnp.where(core == 0, first, second)
        other_ref[rows] = jnp.where(core == 0, second, first)


def pick_columns(place, ids, weights, per_device):
    depth, slab = weights.shape
    tokens = ids.shape[0]
    block = 256
    half = jax.ShapeDtypeStruct((tokens // NC, depth), jnp.bfloat16)
    return pl.pallas_call(
        functools.partial(pick_kernel, per_device),
        grid=(tokens // block,),
        in_specs=[
            SMEM,
            pl.BlockSpec((block, 1), lambda i: (i, 0)),
            pl.BlockSpec((depth, slab), lambda i: (0, 0)),
        ],
        out_specs=[pl.BlockSpec((block // NC, depth), lambda i: (i, 0))] * 2,
        out_shape=[half, half],
        cost_estimate=cost(2 * tokens * depth * slab, 8),
        compiler_params=params(),
    )(place, ids, weights)


def sums_kernel(kind, place_ref, rows_ref, weights_ref, *rest):
    sums_ref = rest[-1]
    z, way = place_ref[0], place_ref[2]
    block = sums_ref.shape[2]
    parts = rows_ref.shape[0] // block
    sums = jnp.dot(rows_ref[...], weights_ref[...], preferred_element_type=jnp.float32)
    for part in range(parts):
        target = pl.program_id(0) * parts + part
        distance = jnp.bitwise_and((target - z) * way, NZ - 1)
        slot = jnp.int32(0)
        for key, value in SLOT_OF.items():
            slot = jnp.where(distance == key, value, slot)
        sums_ref[slot, kind] = sums[part * block : (part + 1) * block]


def partial_sums(place, rows, weights, earlier=None):
    tokens, depth = rows.shape
    slab = weights.shape[1]
    steps = 2
    kind = 0 if earlier is None else 1
    return pl.pallas_call(
        functools.partial(sums_kernel, kind),
        grid=(steps,),
        in_specs=[SMEM, pl.BlockSpec((tokens // steps, depth), lambda i: (i, 0)), VMEM] + [VMEM] * kind,
        out_specs=VMEM,
        out_shape=jax.ShapeDtypeStruct((NZ, NC, tokens // NZ, slab), jnp.float32),
        input_output_aliases={3: 0} if kind else {},
        cost_estimate=cost(2 * tokens * depth * slab, 6),
        compiler_params=params(),
    )(place, rows, weights, *([earlier] if kind else []))


def terms_kernel(heads, per_device, place_ref, own_ref, other_ref, picked_own_ref, picked_other_ref, terms_ref):
    core = place_ref[1]
    tokens, depth = own_ref.shape
    lanes = heads * per_device
    places = tokens // per_device
    head_of = lax.broadcasted_iota(jnp.int32, (depth, lanes), 0) // (depth // heads)
    lane_head = lax.broadcasted_iota(jnp.int32, (depth, lanes), 1) % heads
    spread = (head_of == lane_head).astype(jnp.float32).astype(jnp.bfloat16)
    token = lax.broadcasted_iota(jnp.int32, (places, per_device, lanes), 1)
    lane_token = lax.broadcasted_iota(jnp.int32, (places, per_device, lanes), 2) // heads
    parts = []
    for rows_ref, picked_ref in ((own_ref, picked_own_ref), (other_ref, picked_other_ref)):
        products = rows_ref[...].astype(jnp.float32) * picked_ref[...].astype(jnp.float32)
        high = products.astype(jnp.bfloat16)
        parts += [high, (products - high.astype(jnp.float32)).astype(jnp.bfloat16)]
    sums = jnp.dot(jnp.concatenate(parts, axis=0), spread, preferred_element_type=jnp.float32)
    for kind in range(NC):
        start = 2 * kind * tokens
        terms = sums[start : start + tokens] + sums[start + tokens : start + 2 * tokens]
        terms = jnp.where(token == lane_token, terms.reshape(places, per_device, lanes), 0.0)
        terms_ref[jnp.bitwise_xor(core, kind), :, 0] = jnp.sum(terms, axis=1)


def head_terms(place, own, other, picked_own, picked_other, heads, per_device):
    tokens, depth = own.shape
    lanes = heads * per_device
    steps = 2
    rows = pl.BlockSpec((tokens // steps, depth), lambda i: (i, 0))
    places = tokens // per_device
    return pl.pallas_call(
        functools.partial(terms_kernel, heads, per_device),
        grid=(steps,),
        in_specs=[SMEM, rows, rows, rows, rows],
        out_specs=pl.BlockSpec((NC, places // steps, 1, lanes), lambda i: (0, i, 0, 0)),
        out_shape=jax.ShapeDtypeStruct((NC, places, 1, lanes), jnp.float32),
        cost_estimate=cost(16 * tokens * depth * lanes, 4),
        compiler_params=params(),
    )(place, own, other, picked_own, picked_other)


def eye(size):
    rows = lax.broadcasted_iota(jnp.int32, (size, size), 0)
    return rows == lax.broadcasted_iota(jnp.int32, (size, size), 1)


def stats_kernel(place_ref, logits_ref, terms_ref, message_ref):
    core = place_ref[1]
    found = []
    for kind in range(NC):
        logits = logits_ref[kind]
        top = jnp.max(logits, axis=1, keepdims=True)
        found.append(top + jnp.log(jnp.sum(jnp.exp(logits - top), axis=1, keepdims=True)))
    own, other = found
    lse = jnp.concatenate([jnp.where(core == 0, own, other), jnp.where(core == 0, other, own)], axis=0)
    size = lse.shape[0]
    lse = jnp.sum(jnp.where(eye(size), lse, 0.0), axis=0, keepdims=True)
    terms = jnp.sum(terms_ref[...], axis=0)
    message = jnp.concatenate([lse, terms], axis=0)
    message_ref[...] = jnp.broadcast_to(message[None], message_ref.shape)


def stats(place, logits, terms):
    size = NC * logits.shape[1]
    return pl.pallas_call(
        stats_kernel,
        in_specs=[SMEM, VMEM, VMEM],
        out_specs=VMEM,
        out_shape=jax.ShapeDtypeStruct((NV, 2, size), jnp.float32),
        cost_estimate=cost(0, 1),
        compiler_params=params(),
    )(place, logits, terms)


def finish_kernel(heads, per_device, place_ref, logits_ref, messages_ref, result_ref, attribution_ref, out_ref, semaphore):
    core = place_ref[1]
    every = messages_ref[:, 0, :]
    size = every.shape[1]
    top = jnp.max(every, axis=0, keepdims=True)
    lse = top + jnp.log(jnp.sum(jnp.exp(every - top), axis=0, keepdims=True))
    lse = jnp.sum(jnp.where(eye(size), lse, 0.0), axis=1, keepdims=True)
    half = size // NC
    for c in range(NC):
        logits = logits_ref[jnp.bitwise_xor(core, c)]
        values = (logits - lse[c * half : (c + 1) * half]).astype(out_ref.dtype)
        for place in range(half // per_device):
            start = (place * NC + c) * per_device
            out_ref[start : start + per_device] = values[place * per_device : (place + 1) * per_device]
    copy = pltpu.make_async_copy(out_ref, result_ref, semaphore)
    copy.start()
    shape = (NV, per_device, size)
    token = lax.broadcasted_iota(jnp.int32, shape, 1)
    here = token == lax.broadcasted_iota(jnp.int32, shape, 2) // heads
    head = lax.broadcasted_iota(jnp.int32, (heads, size), 0)
    lane_head = lax.broadcasted_iota(jnp.int32, (heads, size), 1) % heads
    same = (head == lane_head).astype(jnp.float32).astype(jnp.bfloat16)
    left = messages_ref[:, 1, :]
    total = jnp.zeros((heads, NV * per_device), jnp.float32)
    for _ in range(3):
        part = left.astype(jnp.bfloat16).astype(jnp.float32)
        left = left - part
        spread = jnp.where(here, jnp.broadcast_to(part[:, None, :], shape), 0.0)
        spread = spread.reshape(NV * per_device, size).astype(jnp.bfloat16)
        total += lax.dot_general(same, spread, (((1,), (1,)), ((), ())), preferred_element_type=jnp.float32)
    attribution_ref[...] = total
    copy.wait()


def finish(place, logits, messages, heads, per_device):
    tokens, slab = NC * logits.shape[1], logits.shape[2]
    return pl.pallas_call(
        functools.partial(finish_kernel, heads, per_device),
        in_specs=[SMEM, VMEM, VMEM],
        out_specs=[pl.BlockSpec(memory_space=pl.ANY), VMEM],
        out_shape=[
            jax.ShapeDtypeStruct((tokens, slab), jnp.bfloat16),
            jax.ShapeDtypeStruct((heads, NV * per_device), jnp.float32),
        ],
        scratch_shapes=[pltpu.VMEM((tokens, slab), jnp.bfloat16), pltpu.SemaphoreType.DMA],
        cost_estimate=cost(0, 1),
        compiler_params=params(),
    )(place, logits, messages)


def on_device(heads_out, unembed, targets):
    per_device, heads, hd = heads_out.shape
    depth = heads * hd
    slab = unembed.shape[2]
    weights = unembed.reshape(depth, slab)
    vocab_id = lax.axis_index("vocab")
    z = lax.axis_index("head")
    core = vocab_id & 1
    way = 1 - 2 * core
    place = jnp.stack([z, core, way])
    ids = (targets - vocab_id * slab).reshape(-1, 1)
    picked_own, picked_other = pick_columns(place, ids, weights, per_device)
    column = share(heads_out.reshape(per_device, depth), Y_GROUPS, NY)
    own = share(column, X_GROUPS, NX).reshape(-1, depth)
    own = tied(own, picked_own)
    other = lax.ppermute(own, "vocab", CORE_SWAP)
    sums = partial_sums(place, own, weights)
    sums = partial_sums(place, tied(other, sums), weights, sums)

    sent = coded(sums[0])
    four = ring(sent, AHEAD_TWO)
    sent = coded(tied(sums, sent)[2])
    three = ring(sent, AHEAD)
    sent = coded(tied(sums, sent)[1])
    five = ring(sent, BACK)
    sent = coded(tied(sums, sent)[6])
    one = ring(sent, AHEAD)
    terms = head_terms(place, own, tied(other, sent), picked_own, picked_other, heads, per_device)
    sums = tied(sums, terms)
    sent = coded(tied(sums, sent)[5])
    seven = ring(sent, BACK)
    sent = coded(sums[3] + decoded(tied(five, sent)))
    six = ring(sent, BACK_TWO)
    sent = coded(sums[4] + decoded(tied(four, sent)) + decoded(three))
    two = ring(sent, AHEAD_TWO)
    terms = tied(terms, sent).reshape(NV, 1, per_device * heads)
    terms = lax.all_to_all(terms, "vocab", 0, 0, axis_index_groups=CORE_MAJOR, tiled=True)
    part = tied(sums, sent)[7] + decoded(one) + decoded(seven)
    logits = tied(part, sent) + decoded(two) + decoded(six)

    message = stats(place, logits, terms)
    messages = lax.all_to_all(message, "vocab", 0, 0, tiled=True)
    log_probs, attribution = finish(place, logits, messages, heads, per_device)
    return (log_probs, attribution.T)


def solution(mesh):
    in_specs = (P("vocab", "head", None), P("head", None, "vocab"), P())
    out_specs = (P("head", "vocab"), P(None, "head"))
    return jax.shard_map(
        on_device, mesh=mesh, in_specs=in_specs, out_specs=out_specs, check_vma=False
    )
```

```python
import functools

import jax
import jax.numpy as jnp
from jax import lax
from jax.experimental import pallas as pl
from jax.experimental.pallas import tpu as pltpu
from jax.sharding import PartitionSpec as P

NX, NY, NC, NZ = 4, 8, 2, 8
NV = NX * NY * NC
SCALE = 0.125
MIB = 2**20
SLOT_OF = {4: 0, 5: 1, 3: 2, 6: 3, 2: 4, 7: 5, 1: 6, 0: 7}


def vocab_index(x, y, c):
    return (x * NY + y) * NC + c


Y_GROUPS = [[vocab_index(x, y, c) for y in range(NY)] for x in range(NX) for c in range(NC)]
X_GROUPS = [[vocab_index(x, y, c) for x in range(NX)] for y in range(NY) for c in range(NC)]
CORE_MAJOR = [[vocab_index(x, y, c) for c in range(NC) for x in range(NX) for y in range(NY)]]
CORE_SWAP = [(v, v ^ 1) for v in range(NV)]


def hop(sign):
    pairs = []
    for z in range(NZ):
        for v in range(NV):
            step = sign if v % NC == 0 else -sign
            pairs.append((z * NV + v, (z + step) % NZ * NV + v))
    return pairs


AHEAD, BACK, AHEAD_TWO, BACK_TWO = hop(1), hop(-1), hop(2), hop(-2)


def share(block, groups, count):
    copies = jnp.broadcast_to(block[None], (count,) + block.shape)
    return lax.all_to_all(copies, "vocab", 0, 0, axis_index_groups=groups, tiled=True)


def coded(values):
    return (values * SCALE).astype(jnp.float16)


def decoded(values):
    return values.astype(jnp.float32) * (1.0 / SCALE)


def ring(values, pairs):
    return lax.ppermute(values, ("head", "vocab"), pairs)


def tied(value, earlier):
    return lax.optimization_barrier((value, earlier))[0]


def cost(flops, mib):
    return pl.CostEstimate(flops=flops, bytes_accessed=mib * MIB, transcendentals=0)


def params():
    return pltpu.CompilerParams(vmem_limit_bytes=20 * MIB)


SMEM = pl.BlockSpec(memory_space=pltpu.SMEM)
VMEM = pl.BlockSpec(memory_space=pltpu.VMEM)


def pick_kernel(per_device, place_ref, ids_ref, weights_ref, own_ref, other_ref):
    tokens, slab = ids_ref.shape[0], weights_ref.shape[1]
    core = place_ref[1]
    lanes = lax.broadcasted_iota(jnp.int32, (tokens, slab), 1)
    chosen = (ids_ref[...] == lanes).astype(jnp.float32).astype(jnp.bfloat16)
    picked = lax.dot_general(
        chosen, weights_ref[...], (((1,), (1,)), ((), ())), preferred_element_type=jnp.float32
    ).astype(jnp.bfloat16)
    for place in range(tokens // per_device // NC):
        first = picked[2 * place * per_device : (2 * place + 1) * per_device]
        second = picked[(2 * place + 1) * per_device : (2 * place + 2) * per_device]
        rows = slice(place * per_device, (place + 1) * per_device)
        own_ref[rows] = jnp.where(core == 0, first, second)
        other_ref[rows] = jnp.where(core == 0, second, first)


def pick_columns(place, ids, weights, per_device):
    depth, slab = weights.shape
    tokens = ids.shape[0]
    block = 256
    half = jax.ShapeDtypeStruct((tokens // NC, depth), jnp.bfloat16)
    return pl.pallas_call(
        functools.partial(pick_kernel, per_device),
        grid=(tokens // block,),
        in_specs=[
            SMEM,
            pl.BlockSpec((block, 1), lambda i: (i, 0)),
            pl.BlockSpec((depth, slab), lambda i: (0, 0)),
        ],
        out_specs=[pl.BlockSpec((block // NC, depth), lambda i: (i, 0))] * 2,
        out_shape=[half, half],
        cost_estimate=cost(2 * tokens * depth * slab, 8),
        compiler_params=params(),
    )(place, ids, weights)


def sums_kernel(kind, place_ref, rows_ref, weights_ref, *rest):
    sums_ref = rest[-1]
    z, way = place_ref[0], place_ref[2]
    block = sums_ref.shape[2]
    parts = rows_ref.shape[0] // block
    sums = jnp.dot(rows_ref[...], weights_ref[...], preferred_element_type=jnp.float32)
    for part in range(parts):
        target = pl.program_id(0) * parts + part
        distance = jnp.bitwise_and((target - z) * way, NZ - 1)
        slot = jnp.int32(0)
        for key, value in SLOT_OF.items():
            slot = jnp.where(distance == key, value, slot)
        sums_ref[slot, kind] = sums[part * block : (part + 1) * block]


def partial_sums(place, rows, weights, earlier=None):
    tokens, depth = rows.shape
    slab = weights.shape[1]
    steps = 2
    kind = 0 if earlier is None else 1
    return pl.pallas_call(
        functools.partial(sums_kernel, kind),
        grid=(steps,),
        in_specs=[SMEM, pl.BlockSpec((tokens // steps, depth), lambda i: (i, 0)), VMEM] + [VMEM] * kind,
        out_specs=VMEM,
        out_shape=jax.ShapeDtypeStruct((NZ, NC, tokens // NZ, slab), jnp.float32),
        input_output_aliases={3: 0} if kind else {},
        cost_estimate=cost(2 * tokens * depth * slab, 6),
        compiler_params=params(),
    )(place, rows, weights, *([earlier] if kind else []))


def terms_kernel(heads, per_device, place_ref, own_ref, other_ref, picked_own_ref, picked_other_ref, terms_ref):
    core = place_ref[1]
    tokens, depth = own_ref.shape
    lanes = heads * per_device
    places = tokens // per_device
    head_of = lax.broadcasted_iota(jnp.int32, (depth, lanes), 0) // (depth // heads)
    lane_head = lax.broadcasted_iota(jnp.int32, (depth, lanes), 1) % heads
    spread = (head_of == lane_head).astype(jnp.float32).astype(jnp.bfloat16)
    token = lax.broadcasted_iota(jnp.int32, (places, per_device, lanes), 1)
    lane_token = lax.broadcasted_iota(jnp.int32, (places, per_device, lanes), 2) // heads
    parts = []
    for rows_ref, picked_ref in ((own_ref, picked_own_ref), (other_ref, picked_other_ref)):
        products = rows_ref[...].astype(jnp.float32) * picked_ref[...].astype(jnp.float32)
        high = products.astype(jnp.bfloat16)
        parts += [high, (products - high.astype(jnp.float32)).astype(jnp.bfloat16)]
    sums = jnp.dot(jnp.concatenate(parts, axis=0), spread, preferred_element_type=jnp.float32)
    for kind in range(NC):
        start = 2 * kind * tokens
        terms = sums[start : start + tokens] + sums[start + tokens : start + 2 * tokens]
        terms = jnp.where(token == lane_token, terms.reshape(places, per_device, lanes), 0.0)
        terms_ref[jnp.bitwise_xor(core, kind), :, 0] = jnp.sum(terms, axis=1)


def head_terms(place, own, other, picked_own, picked_other, heads, per_device):
    tokens, depth = own.shape
    lanes = heads * per_device
    steps = 2
    rows = pl.BlockSpec((tokens // steps, depth), lambda i: (i, 0))
    places = tokens // per_device
    return pl.pallas_call(
        functools.partial(terms_kernel, heads, per_device),
        grid=(steps,),
        in_specs=[SMEM, rows, rows, rows, rows],
        out_specs=pl.BlockSpec((NC, places // steps, 1, lanes), lambda i: (0, i, 0, 0)),
        out_shape=jax.ShapeDtypeStruct((NC, places, 1, lanes), jnp.float32),
        cost_estimate=cost(16 * tokens * depth * lanes, 4),
        compiler_params=params(),
    )(place, own, other, picked_own, picked_other)


def eye(size):
    rows = lax.broadcasted_iota(jnp.int32, (size, size), 0)
    return rows == lax.broadcasted_iota(jnp.int32, (size, size), 1)


def stats_kernel(place_ref, logits_ref, terms_ref, message_ref):
    core = place_ref[1]
    found = []
    for kind in range(NC):
        logits = logits_ref[kind]
        top = jnp.max(logits, axis=1, keepdims=True)
        found.append(top + jnp.log(jnp.sum(jnp.exp(logits - top), axis=1, keepdims=True)))
    own, other = found
    lse = jnp.concatenate([jnp.where(core == 0, own, other), jnp.where(core == 0, other, own)], axis=0)
    size = lse.shape[0]
    lse = jnp.sum(jnp.where(eye(size), lse, 0.0), axis=0, keepdims=True)
    terms = jnp.sum(terms_ref[...], axis=0)
    message = jnp.concatenate([lse, terms], axis=0)
    message_ref[...] = jnp.broadcast_to(message[None], message_ref.shape)


def stats(place, logits, terms):
    size = NC * logits.shape[1]
    return pl.pallas_call(
        stats_kernel,
        in_specs=[SMEM, VMEM, VMEM],
        out_specs=VMEM,
        out_shape=jax.ShapeDtypeStruct((NV, 2, size), jnp.float32),
        cost_estimate=cost(0, 1),
        compiler_params=params(),
    )(place, logits, terms)


def finish_kernel(heads, per_device, place_ref, logits_ref, messages_ref, out_ref, attribution_ref):
    core = place_ref[1]
    every = messages_ref[:, 0, :]
    size = every.shape[1]
    top = jnp.max(every, axis=0, keepdims=True)
    lse = top + jnp.log(jnp.sum(jnp.exp(every - top), axis=0, keepdims=True))
    lse = jnp.sum(jnp.where(eye(size), lse, 0.0), axis=1, keepdims=True)
    half = size // NC
    for c in range(NC):
        logits = logits_ref[jnp.bitwise_xor(core, c)]
        values = (logits - lse[c * half : (c + 1) * half]).astype(out_ref.dtype)
        for place in range(half // per_device):
            start = (place * NC + c) * per_device
            out_ref[start : start + per_device] = values[place * per_device : (place + 1) * per_device]
    terms = messages_ref[:, 1, :]
    shape = (NV, per_device, size)
    token = lax.broadcasted_iota(jnp.int32, shape, 1)
    lane_token = lax.broadcasted_iota(jnp.int32, shape, 2) // heads
    terms = jnp.where(token == lane_token, jnp.broadcast_to(terms[:, None, :], shape), 0.0)
    head = lax.broadcasted_iota(jnp.int32, (heads, size), 0)
    lane_head = lax.broadcasted_iota(jnp.int32, (heads, size), 1) % heads
    attribution_ref[...] = lax.dot_general(
        (head == lane_head).astype(jnp.float32),
        terms.reshape(NV * per_device, size),
        (((1,), (1,)), ((), ())),
        preferred_element_type=jnp.float32,
        precision=lax.Precision.HIGHEST,
    )


def finish(place, logits, messages, heads, per_device):
    tokens, slab = NC * logits.shape[1], logits.shape[2]
    return pl.pallas_call(
        functools.partial(finish_kernel, heads, per_device),
        in_specs=[SMEM, VMEM, VMEM],
        out_specs=[VMEM, VMEM],
        out_shape=[
            jax.ShapeDtypeStruct((tokens, slab), jnp.bfloat16),
            jax.ShapeDtypeStruct((heads, NV * per_device), jnp.float32),
        ],
        cost_estimate=cost(0, 1),
        compiler_params=params(),
    )(place, logits, messages)


def on_device(heads_out, unembed, targets):
    per_device, heads, hd = heads_out.shape
    depth = heads * hd
    slab = unembed.shape[2]
    weights = unembed.reshape(depth, slab)
    vocab_id = lax.axis_index("vocab")
    z = lax.axis_index("head")
    core = vocab_id & 1
    way = 1 - 2 * core
    place = jnp.stack([z, core, way])
    ids = (targets - vocab_id * slab).reshape(-1, 1)
    picked_own, picked_other = pick_columns(place, ids, weights, per_device)
    column = share(heads_out.reshape(per_device, depth), Y_GROUPS, NY)
    own = share(column, X_GROUPS, NX).reshape(-1, depth)
    own = tied(own, picked_own)
    other = lax.ppermute(own, "vocab", CORE_SWAP)
    sums = partial_sums(place, own, weights)
    sums = partial_sums(place, tied(other, sums), weights, sums)

    sent = coded(sums[2])
    three = ring(sent, AHEAD)
    sent = coded(tied(sums, sent)[0])
    four = ring(sent, AHEAD_TWO)
    sent = coded(tied(sums, sent)[1])
    five = ring(sent, BACK)
    sent = coded(tied(sums, sent)[6])
    one = ring(sent, AHEAD)
    terms = head_terms(place, own, tied(other, sent), picked_own, picked_other, heads, per_device)
    sums = tied(sums, terms)
    sent = coded(tied(sums, sent)[5])
    seven = ring(sent, BACK)
    sent = coded(sums[4] + decoded(tied(four, sent)) + decoded(three))
    two = ring(sent, AHEAD_TWO)
    sent = coded(sums[3] + decoded(tied(five, sent)))
    six = ring(sent, BACK_TWO)
    terms = tied(terms, sent).reshape(NV, 1, per_device * heads)
    terms = lax.all_to_all(terms, "vocab", 0, 0, axis_index_groups=CORE_MAJOR, tiled=True)
    part = tied(sums, sent)[7] + decoded(one) + decoded(seven)
    sent = tied(sent, part)
    logits = part + decoded(two) + decoded(six)

    message = stats(place, logits, terms)
    messages = lax.all_to_all(message, "vocab", 0, 0, tiled=True)
    log_probs, attribution = finish(place, logits, messages, heads, per_device)
    return (log_probs, attribution.T)


def solution(mesh):
    in_specs = (P("vocab", "head", None), P("head", None, "vocab"), P())
    out_specs = (P("head", "vocab"), P(None, "head"))
    return jax.shard_map(
        on_device, mesh=mesh, in_specs=in_specs, out_specs=out_specs, check_vma=False
    )
```
